512 devices in a mesh: lon: 32 (over z_hi, y, core), lat: 16 (over z_lo, x).
Axes of the slice: x: 4, y: 8, z: 8 (z_hi: 2, z_lo: 4; z = z_hi * 4 + z_lo), core: 2. Of those that a mesh axis runs over, the one named last changes fastest.
Arguments:
- ocean_state: float32 [3, 8, 256, 4096], P(None, None, 'lat', 'lon'), may hold values from -6 to 6
- diffusivity: float32 [8, 256, 4096], P(None, 'lat', 'lon'), may hold values from 0.02 to 0.22
- depth_levels: int32 [256, 4096], P('lat', 'lon'), may hold values from 0 to 8, as said below
- fold_pair: int32 [4096], replicated, may hold values from 0 to 4095, as said below
- first_weight: bfloat16 [9, 64, 24], replicated, may hold values from -0.4375 to 0.4375
- mix_weight: bfloat16 [64, 64], replicated, may hold values from -0.75 to 0.75
- last_weight: bfloat16 [9, 16, 64], replicated, may hold values from -0.25 to 0.25
- cotangent: bfloat16 [16, 256, 4096], P(None, 'lat', 'lon'), may hold values from -6 to 6
- active_index: int32 [8192], replicated, may hold values from 0 to 27135, as said below
Outputs:
- new_state: float32 [3, 8, 256, 4096], P(None, None, 'lat', 'lon')
- closure: bfloat16 [16, 256, 4096], P(None, 'lat', 'lon')
- grad_active: float32 [8192], replicated
The draws below stay inside these ranges and needn't reach their ends.
Inputs may be any that keep to these rules, and one draw needn't show every extreme that they name: `depth_levels`: 0 marks land; otherwise the number of wet levels of the column. fold_pair[i] = (s - i) mod 4096 for one s, the same for every i. `active_index`: distinct entries; 0 and 27135 are always among them.
All inputs are finite; a program needn't handle non-finite values.
Results may differ from the reference program's by a relative error of at most 0.0065.
Values may be sent and summed in bfloat16 or wider, within the bound.
No kernel may reach another device: no remote copies, remote signals or barrier semaphores. Data moves between devices by JAX's collectives and lax.ppermute only.
A program may use at most 64 MiB of HBM per device.

```python
import math
import jax
import jax.numpy as jnp
from jax import lax

LEVELS = 8
CHANNELS = 64
LAT_DEV = 16
ACTIVE = 8192
NY = 256
NX = 4096
PARAMS = 27136
N_LAT = 16


def draw_ocean_state(key, part):
    key = jax.random.fold_in(key, 41)
    noise_key = jax.random.fold_in(key, 0)
    noise = jax.random.normal(noise_key, (3, LEVELS, NY, NX), jnp.float32)
    values = noise
    return jnp.clip(values, -6.0, 6.0).astype(jnp.float32)


def draw_diffusivity(key, part):
    key = jax.random.fold_in(key, 43)
    exponent = jax.random.uniform(key, (LEVELS, NY, NX), jnp.float32, math.log(0.02), math.log(0.22))
    values = jnp.exp(exponent)
    return jnp.clip(values, 0.02, 0.22).astype(jnp.float32)


def draw_depth_levels(key, part):
    key = jax.random.fold_in(key, 11)
    land_key, depth_key = jax.random.split(key)
    coast = jax.random.randint(land_key, (NY, NX), 0, 10)
    depth = jax.random.randint(depth_key, (NY, NX), 1, LEVELS + 1)
    return jnp.where(coast < 3, 0, depth).astype(jnp.int32)


def draw_fold_pair(key, part):
    key = jax.random.fold_in(key, 23)
    offset = jax.random.randint(key, (), 0, NX)
    return ((offset - jnp.arange(NX, dtype=jnp.int32)) % NX).astype(jnp.int32)


def draw_active_index(key, part):
    key = jax.random.fold_in(key, 37)
    first_key, order_key = jax.random.split(key)
    inner = jax.random.permutation(first_key, PARAMS - 2)[:ACTIVE - 2].astype(jnp.int32) + 1
    chosen = jnp.concatenate([inner, jnp.array([0, PARAMS - 1], jnp.int32)])
    return jax.random.permutation(order_key, chosen).astype(jnp.int32)


def shard_levels(own_key, shape, pieces, smallest, largest):
    level, own = 1.0, jax.random.fold_in(own_key, 6)
    for axis_at, shards_of in pieces:
        draws = jnp.exp(jax.random.uniform(jax.random.fold_in(own, axis_at), (shards_of,), jnp.float32, smallest / len(pieces), largest / len(pieces)))
        level = level * jnp.repeat(draws, shape[axis_at] // shards_of).reshape([-1 if axis == axis_at else 1 for axis in range(len(shape))])
    return level


def bell_draw(stream_key, extent, scale, reach, cuts=(), held_as=jnp.bfloat16):
    factor_of = shard_levels(stream_key, extent, cuts, -0.22, 0.18) if cuts else 1.0
    result = jax.random.normal(stream_key, extent, jnp.float32) * scale * factor_of
    return jnp.minimum(jnp.maximum(result, -reach), reach).astype(held_as)


def setup_inputs(seed: int = 0) -> dict:
    streams_of = jax.random.split(jax.random.key(seed), 10)
    ocean_state = draw_ocean_state(jax.random.fold_in(streams_of[9], 71), 0)
    diffusivity = draw_diffusivity(jax.random.fold_in(streams_of[9], 71), 0)
    depth_levels = draw_depth_levels(jax.random.fold_in(streams_of[9], 71), 0)
    fold_pair = draw_fold_pair(jax.random.fold_in(streams_of[9], 71), 0)
    first_weight = bell_draw(streams_of[4], (9, CHANNELS, 3 * LEVELS), (27 * LEVELS) ** -0.5, 0.4375)
    mix_weight = bell_draw(streams_of[5], (CHANNELS, CHANNELS), CHANNELS ** -0.5, 0.75)
    last_weight = bell_draw(streams_of[6], (9, 2 * LEVELS, CHANNELS), (9 * CHANNELS) ** -0.5, 0.25)
    cotangent = bell_draw(streams_of[7], (2 * LEVELS, NY, NX), 1.0, 6.0, ((1, 16), (2, 32)))
    active_index = draw_active_index(jax.random.fold_in(streams_of[9], 71), 0)
    return {"ocean_state": ocean_state, "diffusivity": diffusivity, "depth_levels": depth_levels, "fold_pair": fold_pair, "first_weight": first_weight, "mix_weight": mix_weight, "last_weight": last_weight, "cotangent": cotangent, "active_index": active_index}


coriolis_peak = 0.25
pressure_scale = 0.05
advect_scale = 0.25
highest = lax.Precision.HIGHEST

def coriolis(row_ids, row_total):
    mirrored = jnp.where(row_ids >= row_total, 2 * row_total - 1 - row_ids, row_ids)
    return coriolis_peak * jnp.sin(math.pi * (mirrored.astype(jnp.float32) + 0.5) / row_total - 0.5 * math.pi)

def offset_view(field, shift_row, shift_col):
    height = field.shape[1] - 2
    width = field.shape[2] - 2
    return field[:, 1 + shift_row:1 + shift_row + height, 1 + shift_col:1 + shift_col + width]

def stencil(padded, coriolis_rows):
    u_all = padded[0]
    v_all = padded[1]
    t_all = padded[2]
    k_all = padded[3]
    k_center = offset_view(k_all, 0, 0)
    k_east = jnp.sqrt(k_center * offset_view(k_all, 0, 1))
    k_west = jnp.sqrt(k_center * offset_view(k_all, 0, -1))
    k_north = jnp.sqrt(k_center * offset_view(k_all, 1, 0))
    k_south = jnp.sqrt(k_center * offset_view(k_all, -1, 0))

    def diffuse(field):
        middle = offset_view(field, 0, 0)
        return k_east * (offset_view(field, 0, 1) - middle) + k_west * (offset_view(field, 0, -1) - middle) + k_north * (offset_view(field, 1, 0) - middle) + k_south * (offset_view(field, -1, 0) - middle)
    pressure = pressure_scale * jnp.cumsum(t_all, axis=0)
    wet_here = (k_center > 0).astype(jnp.float32)
    f_rows = coriolis_rows[None, :, None]
    u_mid = offset_view(u_all, 0, 0)
    v_mid = offset_view(v_all, 0, 0)
    t_mid = offset_view(t_all, 0, 0)
    u_change = f_rows * v_mid - 0.5 * (offset_view(pressure, 0, 1) - offset_view(pressure, 0, -1))
    v_change = -f_rows * u_mid - 0.5 * (offset_view(pressure, 1, 0) - offset_view(pressure, -1, 0))
    t_change = -advect_scale * 0.5 * (u_mid * (offset_view(t_all, 0, 1) - offset_view(t_all, 0, -1)) + v_mid * (offset_view(t_all, 1, 0) - offset_view(t_all, -1, 0)))
    return jnp.stack([wet_here * (u_mid + u_change + diffuse(u_all)), wet_here * (v_mid + v_change + diffuse(v_all)), wet_here * (t_mid + t_change + diffuse(t_all))])

def pad_fold(field, fold_signs, fold_pair):
    col_total = field.shape[2]
    col_ids = ((jnp.arange(col_total + 2, dtype=jnp.int32) - 1) % col_total).astype(jnp.int32)
    wrapped = jnp.take(field, col_ids, axis=2)
    partner = jnp.take(fold_pair, col_ids).astype(jnp.int32)
    north_rows = fold_signs[:, None] * jnp.take(field[:, -1, :], partner, axis=1)
    south_rows = jnp.zeros_like(north_rows)
    return jnp.concatenate([south_rows[:, None], wrapped, north_rows[:, None]], axis=1)

def pad_open(field):
    col_total = field.shape[2]
    col_ids = ((jnp.arange(col_total + 2, dtype=jnp.int32) - 1) % col_total).astype(jnp.int32)
    wrapped = jnp.take(field, col_ids, axis=2)
    empty_row = jnp.zeros((field.shape[0], 1, col_total + 2), field.dtype)
    return jnp.concatenate([empty_row, wrapped, empty_row], axis=1)

def convolve(padded, weight):
    height = padded.shape[1] - 2
    width = padded.shape[2] - 2
    summed = None
    for tap_index in range(9):
        tap_row = tap_index // 3
        tap_col = tap_index % 3
        term = jnp.einsum('oc,cyx->oyx', weight[tap_index].astype(jnp.float32), padded[:, tap_row:tap_row + height, tap_col:tap_col + width].astype(jnp.float32), precision=highest)
        summed = term if tap_index == 0 else summed + term
    return summed

def convolve_back(padded, weight):
    height = padded.shape[1] - 2
    width = padded.shape[2] - 2
    summed = None
    for tap_index in range(9):
        tap_row = tap_index // 3
        tap_col = tap_index % 3
        term = jnp.einsum('oc,oyx->cyx', weight[tap_index].astype(jnp.float32), padded[:, 2 - tap_row:2 - tap_row + height, 2 - tap_col:2 - tap_col + width].astype(jnp.float32), precision=highest)
        summed = term if tap_index == 0 else summed + term
    return summed

def tap_grads(grad, padded):
    height = grad.shape[1]
    width = grad.shape[2]
    terms = []
    for tap_index in range(9):
        tap_row = tap_index // 3
        tap_col = tap_index % 3
        terms.append(jnp.einsum('oyx,cyx->oc', grad.astype(jnp.float32), padded[:, tap_row:tap_row + height, tap_col:tap_col + width].astype(jnp.float32), precision=highest))
    return jnp.stack(terms)

def silu_slope(pre):
    sigma = jax.nn.sigmoid(pre)
    return sigma * (1.0 + pre * (1.0 - sigma))

def reference(ocean_state, diffusivity, depth_levels, fold_pair, first_weight, mix_weight, last_weight, cotangent, active_index):
    level_ids = jnp.arange(LEVELS, dtype=jnp.int32)
    wet_mask = (level_ids[:, None, None] < depth_levels[None]).astype(jnp.float32)
    wet_kappa = diffusivity * wet_mask
    fields = ocean_state * wet_mask[None]
    fold_signs = jnp.concatenate([-jnp.ones((2 * LEVELS,), jnp.float32), jnp.ones((2 * LEVELS,), jnp.float32)])
    row_ids = jnp.arange(NY, dtype=jnp.int32)
    for step_index in range(2):
        stacked = jnp.concatenate([fields, wet_kappa[None]], axis=0).reshape(4 * LEVELS, NY, NX)
        padded = pad_fold(stacked, fold_signs, fold_pair).reshape(4, LEVELS, NY + 2, NX + 2)
        fields = stencil(padded, coriolis(row_ids, NY))
    new_state = fields
    inputs = new_state.reshape(3 * LEVELS, NY, NX).astype(jnp.bfloat16)
    level_mask = jnp.concatenate([wet_mask, wet_mask], axis=0)
    grad_scale = 1.0 / math.sqrt(NX * NY)
    out_grad = (grad_scale * level_mask * cotangent.astype(jnp.float32)).astype(jnp.bfloat16)
    x_pad = pad_open(inputs)
    g_pad = pad_open(out_grad)
    band_ids = jnp.arange(N_LAT, dtype=jnp.int32)

    def forward_band(band):
        window = lax.dynamic_slice_in_dim(x_pad, band * LAT_DEV, LAT_DEV + 2, 1)
        pre_first = convolve(window, first_weight)
        hidden_first = jax.nn.silu(pre_first).astype(jnp.bfloat16)
        pre_mix = jnp.einsum('oc,cyx->oyx', mix_weight.astype(jnp.float32), hidden_first.astype(jnp.float32), precision=highest)
        hidden_mix = jax.nn.silu(pre_mix).astype(jnp.bfloat16)
        return (window, pre_first, hidden_first, pre_mix, hidden_mix)
    hidden_bands = lax.map(lambda band: forward_band(band)[4], band_ids)
    hidden_all = jnp.transpose(hidden_bands, (1, 0, 2, 3)).reshape(CHANNELS, NY, NX)
    h_pad = pad_open(hidden_all)

    def backward_band(carry, band):
        window, pre_first, hidden_first, pre_mix, hidden_mix = forward_band(band)
        h_window = lax.dynamic_slice_in_dim(h_pad, band * LAT_DEV, LAT_DEV + 2, 1)
        g_window = lax.dynamic_slice_in_dim(g_pad, band * LAT_DEV, LAT_DEV + 2, 1)
        mask_band = lax.dynamic_slice_in_dim(level_mask, band * LAT_DEV, LAT_DEV, 1)
        grad_band = lax.dynamic_slice_in_dim(out_grad, band * LAT_DEV, LAT_DEV, 1)
        closure_band = (mask_band * convolve(h_window, last_weight)).astype(jnp.bfloat16)
        grad_last = tap_grads(grad_band, h_window)
        back_mix = convolve_back(g_window, last_weight)
        delta_mix = (back_mix * silu_slope(pre_mix)).astype(jnp.bfloat16)
        grad_mix = jnp.einsum('oyx,cyx->oc', delta_mix.astype(jnp.float32), hidden_first.astype(jnp.float32), precision=highest)
        back_first = jnp.einsum('oc,oyx->cyx', mix_weight.astype(jnp.float32), delta_mix.astype(jnp.float32), precision=highest)
        delta_first = (back_first * silu_slope(pre_first)).astype(jnp.bfloat16)
        grad_first = tap_grads(delta_first, window)
        return ((carry[0] + grad_first, carry[1] + grad_mix, carry[2] + grad_last), closure_band)
    start = (jnp.zeros((9, CHANNELS, 3 * LEVELS), jnp.float32), jnp.zeros((CHANNELS, CHANNELS), jnp.float32), jnp.zeros((9, 2 * LEVELS, CHANNELS), jnp.float32))
    totals, closure_bands = lax.scan(backward_band, start, band_ids)
    closure = jnp.transpose(closure_bands, (1, 0, 2, 3)).reshape(2 * LEVELS, NY, NX)
    flat = jnp.concatenate([totals[0].reshape(-1), totals[1].reshape(-1), totals[2].reshape(-1)])
    grad_active = jnp.take(flat, active_index.astype(jnp.int32))
    return (new_state, closure, grad_active)
```

```python
import collections
import functools
import math

import jax
import jax.numpy as jnp
import numpy as np
from jax import lax
from jax.experimental import pallas as pl
from jax.experimental.pallas import tpu as pltpu
from jax.sharding import PartitionSpec as P

coriolis_peak = 0.25
pressure_scale = 0.05
advect_scale = 0.25

LEV = 8
ROWS = 16
COLS = 128
HALO = 4
EXT = ROWS + 2 * HALO
WIDE = 2 * COLS
CH = 64
INS = 3 * LEV
OUTS = 2 * LEV
PACK = 48
TAPK = 80
FIRST = 9 * CH * INS
MIX = CH * CH
BOTH = ("lon", "lat")
F32 = jnp.float32
BF16 = jnp.bfloat16


def params(mib=48):
    return pltpu.CompilerParams(vmem_limit_bytes=mib * 1024 * 1024)


def vmem(count):
    return [pl.BlockSpec(memory_space=pltpu.VMEM)] * count


def smem():
    return pl.BlockSpec(memory_space=pltpu.SMEM)


def iota(shape, axis):
    return lax.broadcasted_iota(jnp.int32, shape, axis)


def prep_kernel(grad_scale, state, kappa, depth, cot, own, grad, top, bottom, edges):
    level = iota((LEV, COLS), 0)
    lane = iota((PACK, COLS), 1)
    fields = [jnp.swapaxes(state[f], 0, 1) for f in range(3)]
    kap = jnp.swapaxes(kappa[...], 0, 1)
    cots = jnp.swapaxes(cot[...].astype(F32), 0, 1)
    packed = jnp.zeros((PACK, COLS), F32)
    for r in range(ROWS):
        mask = (level < depth[r : r + 1, :]).astype(F32)
        row = jnp.concatenate([fields[f][r] * mask for f in range(3)] + [kap[r] * mask], axis=0)
        out_grad = grad_scale * jnp.concatenate([mask, mask], axis=0) * cots[r]
        own[r] = row
        grad[r] = out_grad.astype(BF16)
        both = jnp.concatenate([row, out_grad], axis=0)
        if r < HALO:
            bottom[r] = both.astype(BF16)
        if r >= ROWS - HALO:
            top[r - (ROWS - HALO)] = both.astype(BF16)
        moved = pltpu.roll(both, 8 * r, 1) if r else both
        here = ((lane - 8 * r + 4 + COLS) & (COLS - 1)) < 8
        packed = jnp.where(here, moved, packed)
    edges[...] = packed.astype(BF16)


def mid_kernel(scal, own_top, own_bottom, ra, rb, pla, plb, f1, f2, corner):
    core, rel, even = scal[0], scal[1], scal[2]
    lane = iota((PACK, COLS), 1)
    first_core = core == 0
    ea, eb = ra[HALO].astype(F32), rb[HALO].astype(F32)
    east_edge = jnp.where(first_core, ea, eb)
    west_edge = jnp.where(first_core, eb, ea)
    ce = jnp.where((lane & 7) < 4, east_edge, west_edge).astype(BF16)
    corner[...] = ce
    is_even = even == 1
    for k in range(HALO):
        up, down = own_top[k].astype(F32), own_bottom[k].astype(F32)
        pla[k] = jnp.where(is_even, up, down).astype(BF16)
        plb[k] = jnp.where(is_even, down, up).astype(BF16)
    pla[HALO] = ce
    plb[HALO] = ce
    rows_a = ra[:HALO].astype(F32).reshape(HALO * PACK, COLS)
    rows_b = rb[:HALO].astype(F32).reshape(HALO * PACK, COLS)
    west = jnp.where(first_core, rows_b, rows_a).astype(BF16)
    east = jnp.where(first_core, rows_a, rows_b).astype(BF16)
    window = jnp.concatenate([west, own_top[...].reshape(HALO * PACK, COLS), east], axis=1)
    src = iota((3 * COLS, WIDE), 0) - COLS
    t = iota((3 * COLS, WIDE), 1)
    q = t & 7
    target = jnp.where(t < COLS, t, jnp.where(q < 4, COLS + q, q - 8))
    chan = iota((PACK, COLS), 0)
    sign = jnp.where(chan < 2 * LEV, -1.0, jnp.where(chan < 4 * LEV, 1.0, 0.0)).astype(F32)
    slot = ((lane + 4) >> 3) & (ROWS - 1)
    for out, offset, least in ((f1, 0, -COLS), (f2, WIDE, 0)):
        pick = (src == rel - offset - target) & (src >= least)
        moved = jnp.dot(window, pick.astype(F32).astype(BF16), preferred_element_type=F32)
        ext = jnp.zeros((PACK, COLS), F32)
        for k in range(HALO):
            at = (HALO - 1 - k) * PACK
            out[k] = (moved[at : at + PACK, :COLS] * sign).astype(BF16)
            ext = jnp.where(slot == k, moved[at : at + PACK, COLS:], ext)
        out[HALO] = (ext * sign).astype(BF16)


def sigmoid(x):
    return 1.0 / (1.0 + jnp.exp(-x))


def main_kernel(
    scal, spin, valid, own, grad, ce, rla, rlb, rf1, rf2, w1, wm, wmt, wl, wb, hi, lo,
    state_out, closure_out, active_out,
    z0, z1, kxe, kxn, pres, gx, x3, g3, ybuf, acc_first, acc_rest, picked,
):
    even, top = scal[2] == 1, scal[3] == 1

    def place(y, left, corner_pack, slot):
        shift = (COLS - 8 * slot) % COLS
        right = pltpu.roll(corner_pack, shift, 1) if shift else corner_pack
        z0[y, :, :COLS] = left[: 4 * LEV]
        z0[y, :, COLS:] = right[: 4 * LEV]
        gx[y, :, :COLS] = left[4 * LEV :]
        gx[y, :, COLS:] = right[4 * LEV :]

    def south(k):
        return jnp.where(even, rlb[k].astype(F32), rla[k].astype(F32))

    def north(k):
        near = jnp.where(even, rla[k].astype(F32), rlb[k].astype(F32))
        return jnp.where(top, rf1[k].astype(F32) + rf2[k].astype(F32), near)

    south_edge, north_edge, own_edge = south(HALO), north(HALO), ce[...].astype(F32)
    for k in range(HALO):
        place(k, south(k), south_edge, ROWS - HALO + k)
        place(HALO + ROWS + k, north(k), north_edge, k)
    for r in range(ROWS):
        full = jnp.concatenate([own[r], grad[r].astype(F32)], axis=0)
        place(HALO + r, full, own_edge, r)

    def east(x):
        return pltpu.roll(x, WIDE - 1, 1)

    def west(x):
        return pltpu.roll(x, 1, 1)

    level = iota((LEV, WIDE), 0)

    def depth_sum(x):
        for s in (1, 2, 4):
            x = x + jnp.where(level >= s, pltpu.roll(x, s, 0), 0.0)
        return x

    U, V, T, K = (slice(LEV * i, LEV * (i + 1)) for i in range(4))

    def coefficients(y, _):
        k = z0[y, K]
        kxe[y] = jnp.sqrt(k * east(k))
        kxn[y] = jnp.sqrt(k * z0[jnp.minimum(y + 1, EXT - 1), K])
        pres[y] = pressure_scale * depth_sum(z0[y, T])
        return 0

    lax.fori_loop(0, EXT, coefficients, 0, unroll=4)

    def step(src, dst, y):
        ke, kn, ks = kxe[y], kxn[y], kxn[y - 1]
        u, v, t = src[y, U], src[y, V], src[y, T]
        wet = (z0[y, K] > 0).astype(F32)
        f = spin[y]

        def diffuse(z, zn, zs):
            flux = ke * (east(z) - z)
            return flux - west(flux) + kn * (zn - z) + ks * (zs - z)

        p = pres[y]
        un, us = src[y + 1, U], src[y - 1, U]
        vn, vs = src[y + 1, V], src[y - 1, V]
        tn, ts = src[y + 1, T], src[y - 1, T]
        du = f * v - 0.5 * (east(p) - west(p))
        dv = -f * u - 0.5 * (pres[y + 1] - pres[y - 1])
        dt = (-advect_scale * 0.5) * (u * (east(t) - west(t)) + v * (tn - ts))
        dst[y, U] = wet * (u + du + diffuse(u, un, us))
        dst[y, V] = wet * (v + dv + diffuse(v, vn, vs))
        dst[y, T] = wet * (t + dt + diffuse(t, tn, ts))

    def first_step(i, _):
        step(z0, z1, i)
        return 0

    lax.fori_loop(1, EXT - 1, first_step, 0, unroll=2)

    def second_pressure(y, _):
        pres[y] = pressure_scale * depth_sum(z1[y, T])
        return 0

    lax.fori_loop(1, EXT - 1, second_pressure, 0, unroll=2)

    zero_rows = jnp.zeros((TAPK - 3 * INS, WIDE), F32)

    def second_step(y, _):
        step(z1, z0, y)
        x = z0[y, :INS] * valid[y]
        taps = jnp.concatenate([west(x), x, east(x), zero_rows], axis=0)
        x3[pl.ds(pl.multiple_of(TAPK * y, 16), TAPK), :] = taps.astype(BF16)
        g = gx[y]
        tap_g = jnp.concatenate([east(g), g, west(g)], axis=0)[:, :COLS]
        g3[pl.ds(pl.multiple_of(PACK * y, 16), PACK), :] = tap_g.astype(BF16)
        return 0

    lax.fori_loop(2, EXT - 2, second_step, 0, unroll=2)
    new = z0[HALO : HALO + ROWS, :INS, :COLS]
    for f in range(3):
        state_out[f] = jnp.swapaxes(new[:, LEV * f : LEV * (f + 1), :], 0, 1)

    def forward(y):
        taps = x3[pl.ds(pl.multiple_of(TAPK * (y - 1), 16), 3 * TAPK), :]
        pre1 = jnp.dot(w1[...], taps, preferred_element_type=F32)
        s1 = sigmoid(pre1)
        h1 = (pre1 * s1).astype(BF16)
        pre2 = jnp.dot(wm[...], h1, preferred_element_type=F32)
        s2 = sigmoid(pre2)
        h2 = (pre2 * s2 * valid[y]).astype(BF16)
        ybuf[y] = jnp.dot(wl[...], h2, preferred_element_type=F32)
        return taps, pre1, s1, h1, pre2, s2, h2

    forward(HALO - 1)
    forward(HALO + ROWS)
    acc_first[...] = jnp.zeros_like(acc_first)
    acc_rest[...] = jnp.zeros_like(acc_rest)
    nt = (((1,), (1,)), ((), ()))

    def both_ways(i, _):
        y = HALO + i
        taps, pre1, s1, h1, pre2, s2, h2 = (x[:, :COLS] for x in forward(y))
        g9 = g3[pl.ds(pl.multiple_of(PACK * (y - 1), 16), 3 * PACK), :]
        back2 = jnp.dot(wb[...], g9, preferred_element_type=F32)
        d2 = (back2 * (s2 * (1.0 + pre2 * (1.0 - s2)))).astype(BF16)
        back1 = jnp.dot(wmt[...], d2, preferred_element_type=F32)
        d1 = (back1 * (s1 * (1.0 + pre1 * (1.0 - s1)))).astype(BF16)
        acc_first[:, : 3 * TAPK] += lax.dot_general(d1, taps, nt, preferred_element_type=F32)
        gap = jnp.zeros((16, COLS), BF16)
        right = jnp.concatenate([jnp.zeros((160, COLS), BF16), h1, jnp.zeros((32, COLS), BF16)], axis=0)
        left = jnp.concatenate([g9, gap, jnp.zeros((96, COLS), BF16)], axis=0)
        acc_rest[...] += lax.dot_general(h2, left, nt, preferred_element_type=F32) + lax.dot_general(
            d2, right, nt, preferred_element_type=F32
        )
        return 0

    lax.fori_loop(0, ROWS, both_ways, 0)

    closed = []
    for r in range(ROWS):
        y = HALO + r
        part = [
            ybuf[y - 1, OUTS * d : OUTS * (d + 1)]
            + ybuf[y, OUTS * (3 + d) : OUTS * (4 + d)]
            + ybuf[y + 1, OUTS * (6 + d) : OUTS * (7 + d)]
            for d in range(3)
        ]
        total = (west(part[0]) + part[1] + east(part[2]))[:, :COLS]
        wet = (own[r, K] > 0).astype(F32)
        closed.append(jnp.concatenate([wet, wet], axis=0) * total)
    closure_out[...] = jnp.swapaxes(jnp.stack(closed), 0, 1).astype(BF16)

    table = jnp.concatenate([acc_first[...], acc_rest[...]], axis=0).astype(BF16)
    column = iota((WIDE, WIDE), 0)
    line = iota((2 * CH, WIDE), 0)

    def choose(c, _):
        at_hi = jnp.concatenate([hi[pl.ds(2 * c, 1), :], hi[pl.ds(2 * c + 1, 1), :]], axis=1)
        at_lo = jnp.concatenate([lo[pl.ds(2 * c, 1), :], lo[pl.ds(2 * c + 1, 1), :]], axis=1)
        hot = (column == at_hi).astype(F32).astype(BF16)
        found = jnp.dot(table, hot, preferred_element_type=F32)
        value = jnp.sum(jnp.where(line == at_lo, found, 0.0), axis=0, keepdims=True)
        picked[pl.ds(2 * c, 1), :] = value[:, :COLS]
        picked[pl.ds(2 * c + 1, 1), :] = value[:, COLS:]
        return 0

    lax.fori_loop(0, hi.shape[0] // 2, choose, 0, unroll=2)
    active_out[...] = picked[...].astype(BF16)


def swap_pairs(count, start):
    out = []
    for i in range(start, count - 1 + start, 2):
        a, b = i % count, (i + 1) % count
        out += [(a, b), (b, a)]
    return out


def fold_pairs(lon_count, lat_count, q):
    row = lat_count - 1
    return [(i * lat_count + row, ((2 * q - i) % lon_count) * lat_count + row) for i in range(lon_count)]


def groups_of(count, key):
    out = collections.OrderedDict()
    for i in range(count):
        out.setdefault(key(i), []).append(i)
    return list(out.values())


def reduce_over(x, axis, groups):
    count = len(groups[0])
    y = jnp.broadcast_to(x.astype(BF16)[None], (count,) + x.shape)
    y = lax.all_to_all(y, axis, 0, 0, axis_index_groups=groups)
    return jnp.sum(y.astype(F32), axis=0)


def placed_entries(active_index):
    n = active_index
    k, rem = n // (CH * INS), n % (CH * INS)
    hi_a, lo_a = (k // 3) * TAPK + (k % 3) * INS + rem % INS, rem // INS
    g = n - FIRST
    hi_b, lo_b = 160 + g % CH, CH + g // CH
    g = n - FIRST - MIX
    k, rem = g // (OUTS * CH), g % (OUTS * CH)
    hi_c, lo_c = (2 - k // 3) * PACK + (k % 3) * OUTS + rem // CH, CH + rem % CH
    in_a, in_b = n < FIRST, n < FIRST + MIX
    hi = jnp.where(in_a, hi_a, jnp.where(in_b, hi_b, hi_c))
    lo = jnp.where(in_a, lo_a, jnp.where(in_b, lo_b, lo_c))
    return hi.reshape(-1, COLS), lo.reshape(-1, COLS)


def on_device(
    lon_count, lat_count,
    ocean_state, diffusivity, depth_levels, fold_pair, first_weight, mix_weight, last_weight, cotangent, active_index,
):
    lat, lon = lax.axis_index("lat"), lax.axis_index("lon")
    row_total, col_total = ROWS * lat_count, COLS * lon_count
    shape = jax.ShapeDtypeStruct
    own, grad, top, bottom, edges = pl.pallas_call(
        functools.partial(prep_kernel, 1.0 / math.sqrt(row_total * col_total)),
        out_shape=(
            shape((ROWS, 4 * LEV, COLS), F32),
            shape((ROWS, OUTS, COLS), BF16),
            shape((HALO, PACK, COLS), BF16),
            shape((HALO, PACK, COLS), BF16),
            shape((PACK, COLS), BF16),
        ),
        in_specs=vmem(4),
        out_specs=tuple(vmem(5)),
        compiler_params=params(),
        name="prep",
    )(ocean_state, diffusivity, depth_levels, cotangent)

    send = jnp.concatenate([top, edges[None]], axis=0)
    ra = lax.ppermute(send, "lon", swap_pairs(lon_count, 0))
    rb = lax.ppermute(send, "lon", swap_pairs(lon_count, 1) )

    folded = (fold_pair[0] - 3) % col_total
    turn, rel = folded // WIDE, folded % WIDE + 3
    twice = (rel + 4 >= WIDE).astype(jnp.int32)
    scal = jnp.stack(
        [lon % 2, rel, (lat % 2 == 0).astype(jnp.int32), (lat == lat_count - 1).astype(jnp.int32)]
    ).astype(jnp.int32)
    ext_rows = lat * ROWS - HALO + jnp.arange(EXT, dtype=jnp.int32)
    mirrored = jnp.where(ext_rows >= row_total, 2 * row_total - 1 - ext_rows, ext_rows)
    spin = coriolis_peak * jnp.sin(math.pi * (mirrored.astype(F32) + 0.5) / row_total - 0.5 * math.pi)
    valid = ((ext_rows >= 0) & (ext_rows < row_total)).astype(F32)
    hi, lo = placed_entries(active_index)
    w1 = jnp.pad(
        first_weight.reshape(3, 3, CH, INS).transpose(2, 0, 1, 3).reshape(CH, 3, 3 * INS),
        ((0, 0), (0, 0), (0, TAPK - 3 * INS)),
    ).reshape(CH, 3 * TAPK)
    wl = last_weight.reshape(9 * OUTS, CH)
    wb = last_weight.reshape(3, 3, OUTS, CH)[::-1].reshape(9 * OUTS, CH).T
    wmt = mix_weight.T

    block = shape((HALO + 1, PACK, COLS), BF16)
    pla, plb, f1, f2, ce = pl.pallas_call(
        mid_kernel,
        out_shape=(block, block, block, block, shape((PACK, COLS), BF16)),
        in_specs=[smem()] + vmem(4),
        out_specs=tuple(vmem(5)),
        compiler_params=params(),
        name="mid",
    )(scal, top, bottom, ra, rb)

    near_a = swap_pairs(lat_count, 0)
    near_b = swap_pairs(lat_count - 1, 1)

    def exchange(q, second):
        def run(pla, plb, f1, f2):
            rf1 = lax.ppermute(f1, BOTH, fold_pairs(lon_count, lat_count, q))
            if second:
                rf2 = lax.ppermute(f2, BOTH, fold_pairs(lon_count, lat_count, q + 1))
            else:
                rf2 = jnp.zeros_like(f2)
            return lax.ppermute(pla, "lat", near_a), lax.ppermute(plb, "lat", near_b), rf1, rf2

        return run

    turns = lon_count // 2
    branches = [exchange(q, second) for q in range(turns) for second in (False, True)]
    rla, rlb, rf1, rf2 = lax.switch(2 * turn + twice, branches, pla, plb, f1, f2)

    lines = active_index.shape[0] // COLS
    new_state, closure, active = pl.pallas_call(
        main_kernel,
        out_shape=(
            shape((3, LEV, ROWS, COLS), F32),
            shape((OUTS, ROWS, COLS), BF16),
            shape((lines, COLS), BF16),
        ),
        in_specs=[smem()] * 3 + vmem(14),
        out_specs=tuple(vmem(3)),
        scratch_shapes=[
            pltpu.VMEM((EXT, 4 * LEV, WIDE), F32),
            pltpu.VMEM((EXT, 4 * LEV, WIDE), F32),
            pltpu.VMEM((EXT, LEV, WIDE), F32),
            pltpu.VMEM((EXT, LEV, WIDE), F32),
            pltpu.VMEM((EXT, LEV, WIDE), F32),
            pltpu.VMEM((EXT, OUTS, WIDE), F32),
            pltpu.VMEM((EXT * TAPK, WIDE), BF16),
            pltpu.VMEM((EXT * PACK, COLS), BF16),
            pltpu.VMEM((EXT, 9 * OUTS, WIDE), F32),
            pltpu.VMEM((CH, WIDE), F32),
            pltpu.VMEM((CH, WIDE), F32),
            pltpu.VMEM((lines, COLS), F32),
        ],
        compiler_params=params(),
        name="main",
    )(scal, spin, valid, own, grad, ce, rla, rlb, rf1, rf2, w1, mix_weight, wmt, wl, wb, hi, lo)

    total = reduce_over(active, "lat", groups_of(lat_count, lambda i: 0))
    total = reduce_over(total, "lon", groups_of(lon_count, lambda i: i // 16))
    mine = total.astype(BF16)
    half = lon_count // 2
    other = lax.ppermute(mine, "lon", [(i, (i + half) % lon_count) for i in range(lon_count)])
    total = mine.astype(F32) + other.astype(F32)
    return new_state, closure, total.reshape(-1)


def solution(mesh):
    in_specs = (
        P(None, None, "lat", "lon"),
        P(None, "lat", "lon"),
        P("lat", "lon"),
        P(),
        P(),
        P(),
        P(),
        P(None, "lat", "lon"),
        P(),
    )
    out_specs = (P(None, None, "lat", "lon"), P(None, "lat", "lon"), P())
    body = functools.partial(on_device, mesh.shape["lon"], mesh.shape["lat"])
    return jax.shard_map(body, mesh=mesh, in_specs=in_specs, out_specs=out_specs, check_vma=False)
```

```python
import collections
import functools
import math

import jax
import jax.numpy as jnp
from jax import lax
from jax.experimental import pallas as pl
from jax.experimental.pallas import tpu as pltpu
from jax.sharding import PartitionSpec as P

coriolis_peak = 0.25
pressure_scale = 0.05
advect_scale = 0.25

LEV = 8
ROWS = 16
COLS = 128
HALO = 4
EXT = ROWS + 2 * HALO
WIDE = 2 * COLS
CH = 64
INS = 3 * LEV
OUTS = 2 * LEV
PACK = 48
TAPK = 80
FIRST = 9 * CH * INS
MIX = CH * CH
BOTH = ("lon", "lat")
F32 = jnp.float32
BF16 = jnp.bfloat16


def params(mib=48):
    return pltpu.CompilerParams(vmem_limit_bytes=mib * 1024 * 1024)


def vmem(count):
    return [pl.BlockSpec(memory_space=pltpu.VMEM)] * count


def smem():
    return pl.BlockSpec(memory_space=pltpu.SMEM)


def iota(shape, axis):
    return lax.broadcasted_iota(jnp.int32, shape, axis)


def prep_kernel(
    grad_scale, state_hbm, kappa_hbm, depth_hbm, cot_hbm, own, grad, send, bottom, state, kappa, depth, cot, sems
):
    pairs = ((state_hbm, state), (kappa_hbm, kappa), (depth_hbm, depth), (cot_hbm, cot))
    copies = [pltpu.make_async_copy(a, b, sems.at[i]) for i, (a, b) in enumerate(pairs)]
    for copy in copies:
        copy.start()
    for copy in copies:
        copy.wait()
    level = iota((LEV, COLS), 0)
    lane = iota((PACK, COLS), 1)
    fields = [jnp.swapaxes(state[f], 0, 1) for f in range(3)]
    kap = jnp.swapaxes(kappa[...], 0, 1)
    cots = jnp.swapaxes(cot[...].astype(F32), 0, 1)
    packed = jnp.zeros((PACK, COLS), F32)
    for r in range(ROWS):
        mask = (level < depth[r : r + 1, :]).astype(F32)
        row = jnp.concatenate([fields[f][r] * mask for f in range(3)] + [kap[r] * mask], axis=0)
        out_grad = grad_scale * jnp.concatenate([mask, mask], axis=0) * cots[r]
        own[r] = row
        grad[r] = out_grad.astype(BF16)
        both = jnp.concatenate([row, out_grad], axis=0)
        if r < HALO:
            bottom[r] = both.astype(BF16)
        if r >= ROWS - HALO:
            send[r - (ROWS - HALO)] = both.astype(BF16)
        moved = pltpu.roll(both, 8 * r, 1) if r else both
        here = ((lane - 8 * r + 4 + COLS) & (COLS - 1)) < 8
        packed = jnp.where(here, moved, packed)
    send[HALO] = packed.astype(BF16)


def mid_kernel(scal, own_top, own_bottom, rb, ra, pla, plb, plc, corner):
    core, rel, even, at_top = scal[0], scal[1], scal[2], scal[3] == 1
    lane = iota((PACK, COLS), 1)
    first_core = core == 0
    ea, eb = ra[HALO].astype(F32), rb[HALO].astype(F32)
    east_edge = jnp.where(first_core, ea, eb)
    west_edge = jnp.where(first_core, eb, ea)
    ce = jnp.where((lane & 7) < 4, east_edge, west_edge).astype(BF16)
    corner[...] = ce
    is_even = even == 1
    for k in range(HALO):
        up, down = own_top[k].astype(F32), own_bottom[k].astype(F32)
        pla[k] = jnp.where(is_even, up, down).astype(BF16)
        plb[k] = jnp.where(is_even, down, up).astype(BF16)
    pla[HALO] = ce
    plb[HALO] = ce

    @pl.when(jnp.logical_not(at_top))
    def _():
        plc[...] = jnp.zeros_like(plc)

    @pl.when(at_top)
    def _():
        fold_windows(first_core, rel, own_top, ra, rb, plb, plc)


def fold_windows(first_core, rel, own_top, ra, rb, f1, f2):
    lane = iota((PACK, COLS), 1)
    rows_a = ra[:HALO].astype(F32).reshape(HALO * PACK, COLS)
    rows_b = rb[:HALO].astype(F32).reshape(HALO * PACK, COLS)
    west = jnp.where(first_core, rows_b, rows_a).astype(BF16)
    east = jnp.where(first_core, rows_a, rows_b).astype(BF16)
    window = jnp.concatenate([west, own_top[:HALO].reshape(HALO * PACK, COLS), east], axis=1)
    src = iota((3 * COLS, WIDE), 0) - COLS
    t = iota((3 * COLS, WIDE), 1)
    q = t & 7
    target = jnp.where(t < COLS, t, jnp.where(q < 4, COLS + q, q - 8))
    chan = iota((PACK, COLS), 0)
    sign = jnp.where(chan < 2 * LEV, -1.0, jnp.where(chan < 4 * LEV, 1.0, 0.0)).astype(F32)
    slot = ((lane + 4) >> 3) & (ROWS - 1)
    for out, offset, least in ((f1, 0, -COLS), (f2, WIDE, 0)):
        pick = (src == rel - offset - target) & (src >= least)
        moved = jnp.dot(window, pick.astype(F32).astype(BF16), preferred_element_type=F32)
        ext = jnp.zeros((PACK, COLS), F32)
        for k in range(HALO):
            at = (HALO - 1 - k) * PACK
            out[k] = (moved[at : at + PACK, :COLS] * sign).astype(BF16)
            ext = jnp.where(slot == k, moved[at : at + PACK, COLS:], ext)
        out[HALO] = (ext * sign).astype(BF16)


def sigmoid(x):
    return 0.5 * jnp.tanh(0.5 * x) + 0.5


def main_kernel(
    scal, spin, valid, own, grad, ce, rla, rlb, w1, wm, wmt, wl, wb, hi, lo,
    state_out, closure_out, active_out,
    z0, z1, kxe, kxn, pres, gx, x3, g3, ybuf, acc_first, acc_rest, picked,
):
    even = scal[2] == 1

    def place(y, left, corner_pack, slot):
        shift = (COLS - 8 * slot) % COLS
        right = pltpu.roll(corner_pack, shift, 1) if shift else corner_pack
        z0[y, :, :COLS] = left[: 4 * LEV]
        z0[y, :, COLS:] = right[: 4 * LEV]
        gx[y, :, :COLS] = left[4 * LEV :]
        gx[y, :, COLS:] = right[4 * LEV :]

    def south(k):
        return jnp.where(even, rlb[k].astype(F32), rla[k].astype(F32))

    def north(k):
        return jnp.where(even, rla[k].astype(F32), rlb[k].astype(F32))

    south_edge, north_edge, own_edge = south(HALO), north(HALO), ce[...].astype(F32)
    for k in range(HALO):
        place(k, south(k), south_edge, ROWS - HALO + k)
        place(HALO + ROWS + k, north(k), north_edge, k)
    for r in range(ROWS):
        full = jnp.concatenate([own[r], grad[r].astype(F32)], axis=0)
        place(HALO + r, full, own_edge, r)

    def east(x):
        return pltpu.roll(x, WIDE - 1, 1)

    def west(x):
        return pltpu.roll(x, 1, 1)

    level = iota((LEV, WIDE), 0)

    def depth_sum(x):
        for s in (1, 2, 4):
            x = x + jnp.where(level >= s, pltpu.roll(x, s, 0), 0.0)
        return x

    U, V, T, K = (slice(LEV * i, LEV * (i + 1)) for i in range(4))

    def coefficients(y, _):
        k = z0[y, K]
        kxe[y] = jnp.sqrt(k * east(k))
        kxn[y] = jnp.sqrt(k * z0[jnp.minimum(y + 1, EXT - 1), K])
        pres[y] = pressure_scale * depth_sum(z0[y, T])
        return 0

    lax.fori_loop(0, EXT, coefficients, 0, unroll=4)

    def step(src, dst, y):
        ke, kn, ks = kxe[y], kxn[y], kxn[y - 1]
        u, v, t = src[y, U], src[y, V], src[y, T]
        wet = (z0[y, K] > 0).astype(F32)
        f = spin[y]

        def diffuse(z, zn, zs):
            flux = ke * (east(z) - z)
            return flux - west(flux) + kn * (zn - z) + ks * (zs - z)

        p = pres[y]
        un, us = src[y + 1, U], src[y - 1, U]
        vn, vs = src[y + 1, V], src[y - 1, V]
        tn, ts = src[y + 1, T], src[y - 1, T]
        du = f * v - 0.5 * (east(p) - west(p))
        dv = -f * u - 0.5 * (pres[y + 1] - pres[y - 1])
        dt = (-advect_scale * 0.5) * (u * (east(t) - west(t)) + v * (tn - ts))
        dst[y, U] = wet * (u + du + diffuse(u, un, us))
        dst[y, V] = wet * (v + dv + diffuse(v, vn, vs))
        dst[y, T] = wet * (t + dt + diffuse(t, tn, ts))

    def first_step(i, _):
        step(z0, z1, i)
        return 0

    lax.fori_loop(1, EXT - 1, first_step, 0, unroll=11)

    def second_pressure(y, _):
        pres[y] = pressure_scale * depth_sum(z1[y, T])
        return 0

    lax.fori_loop(1, EXT - 1, second_pressure, 0, unroll=2)

    zero_rows = jnp.zeros((TAPK - 3 * INS, WIDE), F32)

    def second_step(y, _):
        step(z1, z0, y)
        x = z0[y, :INS] * valid[y]
        taps = jnp.concatenate([west(x), x, east(x), zero_rows], axis=0)
        x3[pl.ds(pl.multiple_of(TAPK * y, 16), TAPK), :] = taps.astype(BF16)
        g = gx[y]
        tap_g = jnp.concatenate([east(g), g, west(g)], axis=0)[:, :COLS]
        g3[pl.ds(pl.multiple_of(PACK * y, 16), PACK), :] = tap_g.astype(BF16)
        return 0

    lax.fori_loop(2, EXT - 2, second_step, 0, unroll=5)
    new = z0[HALO : HALO + ROWS, :INS, :COLS]
    for f in range(3):
        state_out[f] = jnp.swapaxes(new[:, LEV * f : LEV * (f + 1), :], 0, 1)

    def forward(y):
        taps = x3[pl.ds(pl.multiple_of(TAPK * (y - 1), 16), 3 * TAPK), :]
        pre1 = jnp.dot(w1[...], taps, preferred_element_type=F32)
        s1 = sigmoid(pre1)
        h1 = (pre1 * s1).astype(BF16)
        pre2 = jnp.dot(wm[...], h1, preferred_element_type=F32)
        s2 = sigmoid(pre2)
        h2 = (pre2 * s2 * valid[y]).astype(BF16)
        ybuf[y] = jnp.dot(wl[...], h2, preferred_element_type=F32)
        return taps, pre1, s1, h1, pre2, s2, h2

    forward(HALO - 1)
    forward(HALO + ROWS)
    acc_first[...] = jnp.zeros_like(acc_first)
    acc_rest[...] = jnp.zeros_like(acc_rest)
    nt = (((1,), (1,)), ((), ()))

    def both_ways(i, _):
        y = HALO + i
        taps, pre1, s1, h1, pre2, s2, h2 = (x[:, :COLS] for x in forward(y))
        g9 = g3[pl.ds(pl.multiple_of(PACK * (y - 1), 16), 3 * PACK), :]
        back2 = jnp.dot(wb[...], g9, preferred_element_type=F32)
        d2 = (back2 * (s2 * (1.0 + pre2 * (1.0 - s2)))).astype(BF16)
        back1 = jnp.dot(wmt[...], d2, preferred_element_type=F32)
        d1 = (back1 * (s1 * (1.0 + pre1 * (1.0 - s1)))).astype(BF16)
        acc_first[:, : 3 * TAPK] += lax.dot_general(d1, taps, nt, preferred_element_type=F32)
        gap = jnp.zeros((16, COLS), BF16)
        right = jnp.concatenate([jnp.zeros((160, COLS), BF16), h1, jnp.zeros((32, COLS), BF16)], axis=0)
        left = jnp.concatenate([g9, gap, jnp.zeros((96, COLS), BF16)], axis=0)
        acc_rest[...] += lax.dot_general(h2, left, nt, preferred_element_type=F32) + lax.dot_general(
            d2, right, nt, preferred_element_type=F32
        )
        return 0

    lax.fori_loop(0, ROWS, both_ways, 0, unroll=4)

    closed = []
    for r in range(ROWS):
        y = HALO + r
        part = [
            ybuf[y - 1, OUTS * d : OUTS * (d + 1)]
            + ybuf[y, OUTS * (3 + d) : OUTS * (4 + d)]
            + ybuf[y + 1, OUTS * (6 + d) : OUTS * (7 + d)]
            for d in range(3)
        ]
        total = (west(part[0]) + part[1] + east(part[2]))[:, :COLS]
        wet = (own[r, K] > 0).astype(F32)
        closed.append(jnp.concatenate([wet, wet], axis=0) * total)
    closure_out[...] = jnp.swapaxes(jnp.stack(closed), 0, 1).astype(BF16)

    table = jnp.concatenate([acc_first[...], acc_rest[...]], axis=0).astype(BF16)
    column = iota((WIDE, WIDE), 0)
    line = iota((2 * CH, WIDE), 0)

    def choose(c, _):
        at_hi = jnp.concatenate([hi[pl.ds(2 * c, 1), :], hi[pl.ds(2 * c + 1, 1), :]], axis=1)
        at_lo = jnp.concatenate([lo[pl.ds(2 * c, 1), :], lo[pl.ds(2 * c + 1, 1), :]], axis=1)
        hot = (column == at_hi).astype(F32).astype(BF16)
        found = jnp.dot(table, hot, preferred_element_type=F32)
        value = jnp.sum(jnp.where(line == at_lo, found, 0.0), axis=0, keepdims=True)
        picked[pl.ds(2 * c, 1), :] = value[:, :COLS]
        picked[pl.ds(2 * c + 1, 1), :] = value[:, COLS:]
        return 0

    lax.fori_loop(0, hi.shape[0] // 2, choose, 0, unroll=8)
    active_out[...] = picked[...].astype(BF16)


def swap_pairs(count, start):
    out = []
    for i in range(start, count - 1 + start, 2):
        a, b = i % count, (i + 1) % count
        out += [(a, b), (b, a)]
    return out


def fold_pairs(lon_count, lat_count, q):
    row = lat_count - 1
    return [(i * lat_count + row, ((2 * q - i) % lon_count) * lat_count + row) for i in range(lon_count)]


def groups_of(count, key):
    out = collections.OrderedDict()
    for i in range(count):
        out.setdefault(key(i), []).append(i)
    return list(out.values())


def reduce_over(x, groups):
    count = len(groups[0])
    y = jnp.broadcast_to(x.astype(BF16)[None], (count,) + x.shape)
    y = lax.all_to_all(y, BOTH, 0, 0, axis_index_groups=groups)
    return jnp.sum(y.astype(F32), axis=0)


def placed_entries(active_index):
    n = active_index
    k, rem = n // (CH * INS), n % (CH * INS)
    hi_a, lo_a = (k // 3) * TAPK + (k % 3) * INS + rem % INS, rem // INS
    g = n - FIRST
    hi_b, lo_b = 160 + g % CH, CH + g // CH
    g = n - FIRST - MIX
    k, rem = g // (OUTS * CH), g % (OUTS * CH)
    hi_c, lo_c = (2 - k // 3) * PACK + (k % 3) * OUTS + rem // CH, CH + rem % CH
    in_a, in_b = n < FIRST, n < FIRST + MIX
    hi = jnp.where(in_a, hi_a, jnp.where(in_b, hi_b, hi_c))
    lo = jnp.where(in_a, lo_a, jnp.where(in_b, lo_b, lo_c))
    return hi.reshape(-1, COLS), lo.reshape(-1, COLS)


def run_main(*args):
    shape = jax.ShapeDtypeStruct
    lines = args[-1].shape[0]
    return pl.pallas_call(
        main_kernel,
        out_shape=(
            shape((3, LEV, ROWS, COLS), F32),
            shape((OUTS, ROWS, COLS), BF16),
            shape((lines, COLS), BF16),
        ),
        in_specs=[smem()] * 3 + vmem(12),
        out_specs=tuple(vmem(3)),
        scratch_shapes=[
            pltpu.VMEM((EXT, 4 * LEV, WIDE), F32),
            pltpu.VMEM((EXT, 4 * LEV, WIDE), F32),
            pltpu.VMEM((EXT, LEV, WIDE), F32),
            pltpu.VMEM((EXT, LEV, WIDE), F32),
            pltpu.VMEM((EXT, LEV, WIDE), F32),
            pltpu.VMEM((EXT, OUTS, WIDE), F32),
            pltpu.VMEM((EXT * TAPK, WIDE), BF16),
            pltpu.VMEM((EXT * PACK, COLS), BF16),
            pltpu.VMEM((EXT, 9 * OUTS, WIDE), F32),
            pltpu.VMEM((CH, WIDE), F32),
            pltpu.VMEM((CH, WIDE), F32),
            pltpu.VMEM((lines, COLS), F32),
        ],
        compiler_params=params(),
        name="main",
    )(*args)


def on_device(
    lon_count, lat_count,
    ocean_state, diffusivity, depth_levels, fold_pair, first_weight, mix_weight, last_weight, cotangent, active_index,
):
    lat, lon = lax.axis_index("lat"), lax.axis_index("lon")
    row_total, col_total = ROWS * lat_count, COLS * lon_count
    shape = jax.ShapeDtypeStruct
    block = shape((HALO + 1, PACK, COLS), BF16)
    own, grad, send, bottom = pl.pallas_call(
        functools.partial(prep_kernel, 1.0 / math.sqrt(row_total * col_total)),
        out_shape=(
            shape((ROWS, 4 * LEV, COLS), F32),
            shape((ROWS, OUTS, COLS), BF16),
            block,
            shape((HALO, PACK, COLS), BF16),
        ),
        in_specs=[pl.BlockSpec(memory_space=pltpu.HBM)] * 4,
        out_specs=tuple(vmem(4)),
        scratch_shapes=[
            pltpu.VMEM(x.shape, x.dtype) for x in (ocean_state, diffusivity, depth_levels, cotangent)
        ]
        + [pltpu.SemaphoreType.DMA((4,))],
        compiler_params=params(),
        name="prep",
    )(ocean_state, diffusivity, depth_levels, cotangent)

    rb = lax.ppermute(send, "lon", swap_pairs(lon_count, 1))
    ra = lax.ppermute(send, "lon", swap_pairs(lon_count, 0))

    folded = (fold_pair[0] - 3) % col_total
    turn, rel = folded // WIDE, folded % WIDE + 3
    twice = (rel + 4 >= WIDE).astype(jnp.int32)
    scal = jnp.stack(
        [lon % 2, rel, (lat % 2 == 0).astype(jnp.int32), (lat == lat_count - 1).astype(jnp.int32)]
    ).astype(jnp.int32)
    ext_rows = lat * ROWS - HALO + jnp.arange(EXT, dtype=jnp.int32)
    mirrored = jnp.where(ext_rows >= row_total, 2 * row_total - 1 - ext_rows, ext_rows)
    spin = coriolis_peak * jnp.sin(math.pi * (mirrored.astype(F32) + 0.5) / row_total - 0.5 * math.pi)
    valid = ((ext_rows >= 0) & (ext_rows < row_total)).astype(F32)
    hi, lo = placed_entries(active_index)
    w1 = jnp.pad(
        first_weight.reshape(3, 3, CH, INS).transpose(2, 0, 1, 3).reshape(CH, 3, 3 * INS),
        ((0, 0), (0, 0), (0, TAPK - 3 * INS)),
    ).reshape(CH, 3 * TAPK)
    wl = last_weight.reshape(9 * OUTS, CH)
    wb = last_weight.reshape(3, 3, OUTS, CH)[::-1].reshape(9 * OUTS, CH).T
    wmt = mix_weight.T

    pla, plb, plc, ce = pl.pallas_call(
        mid_kernel,
        out_shape=(block, block, block, shape((PACK, COLS), BF16)),
        in_specs=[smem()] + vmem(4),
        out_specs=tuple(vmem(4)),
        compiler_params=params(),
        name="mid",
    )(scal, send, bottom, rb, ra)

    near_a = [(i * lat_count + a, i * lat_count + b) for i in range(lon_count) for a, b in swap_pairs(lat_count, 0)]
    near_b = [
        (i * lat_count + a, i * lat_count + b) for i in range(lon_count) for a, b in swap_pairs(lat_count - 1, 1)
    ]
    turns = lon_count // 2

    def exchange(q, second):
        def run(pla, plb, plc):
            rlb = lax.ppermute(plb, BOTH, near_b + fold_pairs(lon_count, lat_count, q))
            if second:
                rlb = rlb + lax.ppermute(plc, BOTH, near_b + fold_pairs(lon_count, lat_count, (q + 1) % turns))
            return rlb, lax.ppermute(pla, BOTH, near_a)

        return run

    branches = [exchange(q, second) for q in range(turns) for second in (False, True)]
    rlb, rla = lax.switch(2 * turn + twice, branches, pla, plb, plc)

    new_state, closure, active = run_main(
        scal, spin, valid, own, grad, ce, rla, rlb, w1, mix_weight, wmt, wl, wb, hi, lo
    )

    halves, cores, quads = 2, 2, 4
    inner = lon_count // halves
    everyone = lon_count * lat_count

    def place_of(d):
        lon_at, lat_at = divmod(d, lat_count)
        z_hi, low = divmod(lon_at, inner)
        return z_hi, low // cores, low % cores, lat_at // quads, lat_at % quads

    def grouped(kept):
        return groups_of(everyone, lambda d: tuple(place_of(d)[i] for i in kept))

    total = reduce_over(active, grouped((0, 1, 3)))
    total = reduce_over(total, grouped((0, 2, 3, 4)))
    total = reduce_over(total, grouped((1, 2, 4)))
    return new_state, closure, total.reshape(-1)


def solution(mesh):
    in_specs = (
        P(None, None, "lat", "lon"),
        P(None, "lat", "lon"),
        P("lat", "lon"),
        P(),
        P(),
        P(),
        P(),
        P(None, "lat", "lon"),
        P(),
    )
    out_specs = (P(None, None, "lat", "lon"), P(None, "lat", "lon"), P())
    body = functools.partial(on_device, mesh.shape["lon"], mesh.shape["lat"])
    return jax.shard_map(body, mesh=mesh, in_specs=in_specs, out_specs=out_specs, check_vma=False)
```

```python
import collections
import functools
import math

import jax
import jax.numpy as jnp
from jax import lax
from jax.experimental import pallas as pl
from jax.experimental.pallas import tpu as pltpu
from jax.sharding import PartitionSpec as P

coriolis_peak = 0.25
pressure_scale = 0.05
advect_scale = 0.25

LEV = 8
ROWS = 16
COLS = 128
HALO = 4
EXT = ROWS + 2 * HALO
WIDE = 2 * COLS
CH = 64
INS = 3 * LEV
OUTS = 2 * LEV
PACK = 48
TAPK = 80
FIRST = 9 * CH * INS
MIX = CH * CH
GRANT = 60
SHARE = 8
BOTH = ("lon", "lat")
F32 = jnp.float32
BF16 = jnp.bfloat16


def params(mib=48):
    return pltpu.CompilerParams(vmem_limit_bytes=mib * 1024 * 1024)


def vmem(count):
    return [pl.BlockSpec(memory_space=pltpu.VMEM)] * count


def smem():
    return pl.BlockSpec(memory_space=pltpu.SMEM)


def iota(shape, axis):
    return lax.broadcasted_iota(jnp.int32, shape, axis)


def prep_kernel(
    grad_scale, col_total, lat_count, state_hbm, kappa_hbm, depth_hbm, cot_hbm, fold_hbm,
    own, grad, send, bottom, scal, turn, state, kappa, depth, cot, fold, sems,
):
    lat, lon = lax.axis_index("lat"), lax.axis_index("lon")
    pairs = ((state_hbm, state), (kappa_hbm, kappa), (depth_hbm, depth), (cot_hbm, cot), (fold_hbm, fold))
    copies = [pltpu.make_async_copy(a, b, sems.at[i]) for i, (a, b) in enumerate(pairs)]
    for copy in copies:
        copy.start()
    for copy in copies:
        copy.wait()
    folded = lax.rem(fold[0] + col_total - 3, col_total)
    rel = lax.rem(folded, WIDE) + 3
    scal[0] = lax.rem(lon, 2)
    scal[1] = rel
    scal[2] = (lax.rem(lat, 2) == 0).astype(jnp.int32)
    scal[3] = (lat == lat_count - 1).astype(jnp.int32)
    turn[0] = 2 * lax.div(folded, WIDE) + (rel + 4 >= WIDE).astype(jnp.int32)
    level = iota((LEV, COLS), 0)
    lane = iota((PACK, COLS), 1)
    fields = [jnp.swapaxes(state[f], 0, 1) for f in range(3)]
    kap = jnp.swapaxes(kappa[...], 0, 1)
    cots = jnp.swapaxes(cot[...].astype(F32), 0, 1)
    packed = jnp.zeros((PACK, COLS), F32)
    for r in range(ROWS):
        mask = (level < depth[r : r + 1, :]).astype(F32)
        row = jnp.concatenate([fields[f][r] * mask for f in range(3)] + [kap[r] * mask], axis=0)
        out_grad = grad_scale * jnp.concatenate([mask, mask], axis=0) * cots[r]
        own[r] = row
        grad[r] = out_grad.astype(BF16)
        both = jnp.concatenate([row, out_grad], axis=0)
        if r < HALO:
            bottom[r] = both.astype(BF16)
        if r >= ROWS - HALO:
            send[r - (ROWS - HALO)] = both.astype(BF16)
        moved = pltpu.roll(both, 8 * r, 1) if r else both
        here = ((lane - 8 * r + 4 + COLS) & (COLS - 1)) < 8
        packed = jnp.where(here, moved, packed)
    send[HALO] = packed.astype(BF16)


def mid_kernel(scal, own_top, own_bottom, ra, rb, pla, plb, plc, corner):
    core, rel, even, at_top = scal[0], scal[1], scal[2], scal[3] == 1
    lane = iota((PACK, COLS), 1)
    first_core = core == 0
    ea, eb = ra[HALO].astype(F32), rb[HALO].astype(F32)
    east_edge = jnp.where(first_core, ea, eb)
    west_edge = jnp.where(first_core, eb, ea)
    ce = jnp.where((lane & 7) < 4, east_edge, west_edge).astype(BF16)
    corner[...] = ce
    is_even = even == 1
    for k in range(HALO):
        up, down = own_top[k].astype(F32), own_bottom[k].astype(F32)
        pla[k] = jnp.where(is_even, up, down).astype(BF16)
        plb[k] = jnp.where(is_even, down, up).astype(BF16)
    pla[HALO] = ce
    plb[HALO] = ce

    @pl.when(jnp.logical_not(at_top))
    def _():
        plc[...] = jnp.zeros_like(plc)

    @pl.when(at_top)
    def _():
        fold_windows(first_core, rel, own_top, ra, rb, plb, plc)


def fold_windows(first_core, rel, own_top, ra, rb, f1, f2):
    lane = iota((PACK, COLS), 1)
    rows_a = ra[:HALO].astype(F32).reshape(HALO * PACK, COLS)
    rows_b = rb[:HALO].astype(F32).reshape(HALO * PACK, COLS)
    west = jnp.where(first_core, rows_b, rows_a).astype(BF16)
    east = jnp.where(first_core, rows_a, rows_b).astype(BF16)
    window = jnp.concatenate([west, own_top[:HALO].reshape(HALO * PACK, COLS), east], axis=1)
    src = iota((3 * COLS, WIDE), 0) - COLS
    t = iota((3 * COLS, WIDE), 1)
    q = t & 7
    target = jnp.where(t < COLS, t, jnp.where(q < 4, COLS + q, q - 8))
    chan = iota((PACK, COLS), 0)
    sign = jnp.where(chan < 2 * LEV, -1.0, jnp.where(chan < 4 * LEV, 1.0, 0.0)).astype(F32)
    slot = ((lane + 4) >> 3) & (ROWS - 1)
    for out, offset, least in ((f1, 0, -COLS), (f2, WIDE, 0)):
        pick = (src == rel - offset - target) & (src >= least)
        moved = jnp.dot(window, pick.astype(F32).astype(BF16), preferred_element_type=F32)
        ext = jnp.zeros((PACK, COLS), F32)
        for k in range(HALO):
            at = (HALO - 1 - k) * PACK
            out[k] = (moved[at : at + PACK, :COLS] * sign).astype(BF16)
            ext = jnp.where(slot == k, moved[at : at + PACK, COLS:], ext)
        out[HALO] = (ext * sign).astype(BF16)


def sigmoid(x):
    return 0.5 * jnp.tanh(0.5 * x) + 0.5


def placed_entries(active_index):
    def split(x, by):
        whole = lax.div(x, jnp.full_like(x, by))
        return whole, x - whole * by

    n = active_index
    k, rem = split(n, CH * INS)
    (dy, dx), (o, c) = split(k, 3), split(rem, INS)
    hi_a, lo_a = dy * TAPK + dx * INS + c, o
    o, c = split(n - FIRST, CH)
    hi_b, lo_b = 9 * OUTS + c, CH + o
    k, rem = split(n - FIRST - MIX, OUTS * CH)
    (dy, dx), (o, c) = split(k, 3), split(rem, CH)
    hi_c, lo_c = (2 - dy) * PACK + dx * OUTS + o, CH + c
    in_a, in_b = n < FIRST, n < FIRST + MIX
    hi = jnp.where(in_a, hi_a, jnp.where(in_b, hi_b, hi_c))
    lo = jnp.where(in_a, lo_a, jnp.where(in_b, lo_b, lo_c))
    return hi, lo


def main_kernel(
    row_total, own, grad, ce, rla, rlb, first_hbm, mix_hbm, last_hbm, entries_hbm,
    state_out, closure_out, active_out,
    z0, z1, kxe, kxn, pres, gx, x3, g3, ybuf, acc_first, acc_rest, picked,
    first_taps, mix, last, entries, w1, wmt, wl, wb, hi, lo, spin, sems,
):
    pairs = ((first_hbm, first_taps), (mix_hbm, mix), (last_hbm, last), (entries_hbm, entries))
    copies = [pltpu.make_async_copy(a, b, sems.at[i]) for i, (a, b) in enumerate(pairs)]
    for copy in copies:
        copy.start()
    lat = lax.axis_index("lat")
    even = lax.rem(lat, 2) == 0
    first_row = lat * ROWS - HALO
    at_row = first_row + iota((EXT, COLS), 0)
    mirrored = jnp.where(at_row >= row_total, 2 * row_total - 1 - at_row, at_row)
    spin[...] = coriolis_peak * jnp.sin(math.pi * (mirrored.astype(F32) + 0.5) / row_total - 0.5 * math.pi)

    def valid(y):
        return jnp.where((first_row + y >= 0) & (first_row + y < row_total), 1.0, 0.0)


    def place(y, left, corner_pack, slot):
        shift = (COLS - 8 * slot) % COLS
        right = pltpu.roll(corner_pack, shift, 1) if shift else corner_pack
        z0[y, :, :COLS] = left[: 4 * LEV]
        z0[y, :, COLS:] = right[: 4 * LEV]
        gx[y, :, :COLS] = left[4 * LEV :]
        gx[y, :, COLS:] = right[4 * LEV :]

    def south(k):
        return jnp.where(even, rlb[k].astype(F32), rla[k].astype(F32))

    def north(k):
        return jnp.where(even, rla[k].astype(F32), rlb[k].astype(F32))

    south_edge, north_edge, own_edge = south(HALO), north(HALO), ce[...].astype(F32)
    for k in range(HALO):
        place(k, south(k), south_edge, ROWS - HALO + k)
        place(HALO + ROWS + k, north(k), north_edge, k)
    for r in range(ROWS):
        full = jnp.concatenate([own[r], grad[r].astype(F32)], axis=0)
        place(HALO + r, full, own_edge, r)

    def east(x):
        return pltpu.roll(x, WIDE - 1, 1)

    def west(x):
        return pltpu.roll(x, 1, 1)

    level = iota((LEV, WIDE), 0)

    def depth_sum(x):
        for s in (1, 2, 4):
            x = x + jnp.where(level >= s, pltpu.roll(x, s, 0), 0.0)
        return x

    U, V, T, K = (slice(LEV * i, LEV * (i + 1)) for i in range(4))

    def coefficients(y, _):
        k = z0[y, K]
        kxe[y] = jnp.sqrt(k * east(k))
        kxn[y] = jnp.sqrt(k * z0[jnp.minimum(y + 1, EXT - 1), K])
        pres[y] = pressure_scale * depth_sum(z0[y, T])
        return 0

    lax.fori_loop(0, EXT, coefficients, 0, unroll=4)

    def step(src, dst, y):
        ke, kn, ks = kxe[y], kxn[y], kxn[y - 1]
        u, v, t = src[y, U], src[y, V], src[y, T]
        wet = (z0[y, K] > 0).astype(F32)
        row = spin[pl.ds(y, 1), :]
        f = jnp.concatenate([row, row], axis=1)

        def diffuse(z, zn, zs):
            flux = ke * (east(z) - z)
            return flux - west(flux) + kn * (zn - z) + ks * (zs - z)

        p = pres[y]
        un, us = src[y + 1, U], src[y - 1, U]
        vn, vs = src[y + 1, V], src[y - 1, V]
        tn, ts = src[y + 1, T], src[y - 1, T]
        du = f * v - 0.5 * (east(p) - west(p))
        dv = -f * u - 0.5 * (pres[y + 1] - pres[y - 1])
        dt = (-advect_scale * 0.5) * (u * (east(t) - west(t)) + v * (tn - ts))
        dst[y, U] = wet * (u + du + diffuse(u, un, us))
        dst[y, V] = wet * (v + dv + diffuse(v, vn, vs))
        dst[y, T] = wet * (t + dt + diffuse(t, tn, ts))

    def first_step(i, _):
        step(z0, z1, i)
        return 0

    lax.fori_loop(1, EXT - 1, first_step, 0, unroll=11)

    def second_pressure(y, _):
        pres[y] = pressure_scale * depth_sum(z1[y, T])
        return 0

    lax.fori_loop(1, EXT - 1, second_pressure, 0, unroll=2)

    zero_rows = jnp.zeros((TAPK - 3 * INS, COLS), F32)

    def second_step(y, _):
        step(z1, z0, y)
        x = z0[y, :INS] * valid(y)
        taps = jnp.concatenate([west(x)[:, :COLS], x[:, :COLS], east(x)[:, :COLS], zero_rows], axis=0)
        x3[pl.ds(pl.multiple_of(TAPK * y, 16), TAPK), :] = taps.astype(BF16)
        g = gx[y]
        tap_g = jnp.concatenate([east(g), g, west(g)], axis=0)[:, :COLS]
        g3[pl.ds(pl.multiple_of(PACK * y, 16), PACK), :] = tap_g.astype(BF16)
        return 0

    lax.fori_loop(2, EXT - 2, second_step, 0, unroll=5)
    new = z0[HALO : HALO + ROWS, :INS, :COLS]
    for f in range(3):
        state_out[f] = jnp.swapaxes(new[:, LEV * f : LEV * (f + 1), :], 0, 1)

    for copy in copies:
        copy.wait()
    pieces = []
    for k in range(9):
        pieces.append(first_taps[k].astype(F32))
        if k % 3 == 2:
            pieces.append(jnp.zeros((TAPK - 3 * INS, CH), F32))
    w1[...] = jnp.concatenate(pieces, axis=0).T.astype(BF16)
    wmt[...] = mix[...].astype(F32).T.astype(BF16)
    taps_of = [last[k].astype(F32) for k in range(9)]
    wl[...] = jnp.concatenate(taps_of, axis=0).astype(BF16)
    wb[...] = jnp.concatenate(taps_of[6:] + taps_of[3:6] + taps_of[:3], axis=0).T.astype(BF16)
    hi[...], lo[...] = placed_entries(entries[...])

    def hidden(taps):
        pre1 = jnp.dot(w1[...], taps, preferred_element_type=F32)
        s1 = sigmoid(pre1)
        h1 = (pre1 * s1).astype(BF16)
        pre2 = jnp.dot(mix[...], h1, preferred_element_type=F32)
        s2 = sigmoid(pre2)
        return pre1, s1, h1, pre2, s2, pre2 * s2

    def two_rows(ref, depth, y, z):
        return jnp.concatenate(
            [ref[pl.ds(pl.multiple_of(depth * (r - 1), 16), 3 * depth), :] for r in (y, z)], axis=1
        )

    def spread(h2):
        return jnp.dot(wl[...], h2.astype(BF16), preferred_element_type=F32)

    lane = iota((INS, COLS), 1)
    columns = [jnp.zeros((INS, COLS), F32)] * 3
    for y in range(2, EXT - 2):
        x = z0[y, :INS] * valid(y)
        inner, outer = x[:, :COLS], x[:, COLS:]
        sides = (jnp.where(lane == COLS - 1, inner, outer), outer, jnp.where(lane == 0, inner, outer))
        for d in range(3):
            moved = pltpu.roll(sides[d], 2 * y + 2 - d, 1)
            columns[d] = jnp.where((lane >> 1) == y, moved, columns[d])
    side_taps = []
    for shift in (2, 0, COLS - 2):
        side_taps += [pltpu.roll(c, shift, 1) if shift else c for c in columns] + [zero_rows]
    side_row = first_row + (iota((CH, COLS), 1) >> 1)
    side_valid = ((side_row >= 0) & (side_row < row_total)).astype(F32)
    side = spread(hidden(jnp.concatenate(side_taps, axis=0).astype(BF16))[5] * side_valid)
    side_sum = []
    for d in (0, 2):
        parts = [side[OUTS * (3 * k + d) : OUTS * (3 * k + d + 1)] for k in range(3)]
        side_sum.append(pltpu.roll(parts[0], 2, 1) + parts[1] + pltpu.roll(parts[2], COLS - 2, 1))

    low, high = HALO - 1, HALO + ROWS
    h2 = hidden(two_rows(x3, TAPK, low, high))[5]
    ends = spread(jnp.concatenate([h2[:, :COLS] * valid(low), h2[:, COLS:] * valid(high)], axis=1))
    ybuf[low] = ends[:, :COLS]
    ybuf[high] = ends[:, COLS:]
    acc_first[...] = jnp.zeros_like(acc_first)
    acc_rest[...] = jnp.zeros_like(acc_rest)
    nt = (((1,), (1,)), ((), ()))

    def both_ways(i, _):
        y = HALO + 2 * i
        taps = two_rows(x3, TAPK, y, y + 1)
        pre1, s1, h1, pre2, s2, act = hidden(taps)
        h2 = act.astype(BF16)
        out = spread(h2)
        ybuf[y] = out[:, :COLS]
        ybuf[y + 1] = out[:, COLS:]
        g9 = two_rows(g3, PACK, y, y + 1)
        back2 = jnp.dot(wb[...], g9, preferred_element_type=F32)
        d2 = (back2 * (s2 * (1.0 + pre2 * (1.0 - s2)))).astype(BF16)
        back1 = jnp.dot(wmt[...], d2, preferred_element_type=F32)
        d1 = (back1 * (s1 * (1.0 + pre1 * (1.0 - s1)))).astype(BF16)
        acc_first[:, : 3 * TAPK] += lax.dot_general(d1, taps, nt, preferred_element_type=F32)
        acc_rest[:, : 9 * OUTS + CH] += lax.dot_general(
            jnp.concatenate([h2, d2], axis=0), jnp.concatenate([g9, h1], axis=0), nt, preferred_element_type=F32
        )
        return 0

    lax.fori_loop(0, ROWS // 2, both_ways, 0, unroll=8)

    closed = []
    lane = iota((OUTS, COLS), 1)
    for r in range(ROWS):
        y = HALO + r
        part = [
            ybuf[y - 1, OUTS * d : OUTS * (d + 1)]
            + ybuf[y, OUTS * (3 + d) : OUTS * (4 + d)]
            + ybuf[y + 1, OUTS * (6 + d) : OUTS * (7 + d)]
            for d in range(3)
        ]
        from_west = jnp.where(lane == 0, pltpu.roll(side_sum[0], COLS - 2 * y, 1), pltpu.roll(part[0], 1, 1))
        from_east = jnp.where(
            lane == COLS - 1, pltpu.roll(side_sum[1], COLS - 2 - 2 * y, 1), pltpu.roll(part[2], COLS - 1, 1)
        )
        wet = (own[r, K] > 0).astype(F32)
        closed.append(jnp.concatenate([wet, wet], axis=0) * (from_west + part[1] + from_east))
    closure_out[...] = jnp.swapaxes(jnp.stack(closed), 0, 1).astype(BF16)

    is_last = iota((CH, WIDE), 1) < 9 * OUTS
    rest = jnp.where(is_last, acc_rest[:CH], acc_rest[CH:])
    table = jnp.concatenate([acc_first[...], rest], axis=0).astype(BF16)
    column = iota((WIDE, WIDE), 0)
    line = iota((2 * CH, WIDE), 0)

    def choose(c, _):
        at_hi = jnp.concatenate([hi[pl.ds(2 * c, 1), :], hi[pl.ds(2 * c + 1, 1), :]], axis=1)
        at_lo = jnp.concatenate([lo[pl.ds(2 * c, 1), :], lo[pl.ds(2 * c + 1, 1), :]], axis=1)
        hot = (column == at_hi).astype(F32).astype(BF16)
        found = jnp.dot(table, hot, preferred_element_type=F32)
        value = jnp.sum(jnp.where(line == at_lo, found, 0.0), axis=0, keepdims=True)
        picked[pl.ds(2 * c, 1), :] = value[:, :COLS]
        picked[pl.ds(2 * c + 1, 1), :] = value[:, COLS:]
        return 0

    lax.fori_loop(0, hi.shape[0] // 2, choose, 0, unroll=8)
    chosen = picked[...].astype(BF16)
    for k in range(SHARE):
        active_out[k] = chosen


def swap_pairs(count, start):
    out = []
    for i in range(start, count - 1 + start, 2):
        a, b = i % count, (i + 1) % count
        out += [(a, b), (b, a)]
    return out


def fold_pairs(lon_count, lat_count, q):
    row = lat_count - 1
    return [(i * lat_count + row, ((2 * q - i) % lon_count) * lat_count + row) for i in range(lon_count)]


def groups_of(count, key):
    out = collections.OrderedDict()
    for i in range(count):
        out.setdefault(key(i), []).append(i)
    return list(out.values())


def reduce_over(shares, groups):
    arrived = lax.all_to_all(shares, BOTH, 0, 0, axis_index_groups=groups)
    return jnp.sum(arrived.astype(F32), axis=0)


def shared(x):
    return jnp.broadcast_to(x.astype(BF16)[None], (SHARE,) + x.shape)


def run_main(row_total, *args):
    shape = jax.ShapeDtypeStruct
    lines = args[-1].shape[0]
    return pl.pallas_call(
        functools.partial(main_kernel, row_total),
        out_shape=(
            shape((3, LEV, ROWS, COLS), F32),
            shape((OUTS, ROWS, COLS), BF16),
            shape((SHARE, lines, COLS), BF16),
        ),
        in_specs=vmem(5) + [pl.BlockSpec(memory_space=pltpu.HBM)] * 4,
        out_specs=tuple(vmem(3)),
        scratch_shapes=[
            pltpu.VMEM((EXT, 4 * LEV, WIDE), F32),
            pltpu.VMEM((EXT, 4 * LEV, WIDE), F32),
            pltpu.VMEM((EXT, LEV, WIDE), F32),
            pltpu.VMEM((EXT, LEV, WIDE), F32),
            pltpu.VMEM((EXT, LEV, WIDE), F32),
            pltpu.VMEM((EXT, OUTS, WIDE), F32),
            pltpu.VMEM((EXT * TAPK, COLS), BF16),
            pltpu.VMEM((EXT * PACK, COLS), BF16),
            pltpu.VMEM((EXT, 9 * OUTS, COLS), F32),
            pltpu.VMEM((CH, WIDE), F32),
            pltpu.VMEM((2 * CH, WIDE), F32),
            pltpu.VMEM((lines, COLS), F32),
        ]
        + [pltpu.VMEM(x.shape, x.dtype) for x in args[-4:]]
        + [
            pltpu.VMEM((CH, 3 * TAPK), BF16),
            pltpu.VMEM((CH, CH), BF16),
            pltpu.VMEM((9 * OUTS, CH), BF16),
            pltpu.VMEM((CH, 9 * OUTS), BF16),
            pltpu.VMEM((lines, COLS), jnp.int32),
            pltpu.VMEM((lines, COLS), jnp.int32),
            pltpu.VMEM((EXT, COLS), F32),
            pltpu.SemaphoreType.DMA((4,)),
        ],
        compiler_params=params(GRANT),
        name="main",
    )(*args)


def on_device(
    lon_count, lat_count,
    ocean_state, diffusivity, depth_levels, fold_pair, first_weight, mix_weight, last_weight, cotangent, active_index,
):
    lat, lon = lax.axis_index("lat"), lax.axis_index("lon")
    row_total, col_total = ROWS * lat_count, COLS * lon_count
    shape = jax.ShapeDtypeStruct
    block = shape((HALO + 1, PACK, COLS), BF16)
    own, grad, send, bottom, scal, turn = pl.pallas_call(
        functools.partial(prep_kernel, 1.0 / math.sqrt(row_total * col_total), col_total, lat_count),
        out_shape=(
            shape((ROWS, 4 * LEV, COLS), F32),
            shape((ROWS, OUTS, COLS), BF16),
            block,
            shape((HALO, PACK, COLS), BF16),
            shape((4,), jnp.int32),
            shape((1,), jnp.int32),
        ),
        in_specs=[pl.BlockSpec(memory_space=pltpu.HBM)] * 5,
        out_specs=tuple(vmem(4) + [smem()] * 2),
        scratch_shapes=[
            pltpu.VMEM(x.shape, x.dtype) for x in (ocean_state, diffusivity, depth_levels, cotangent)
        ]
        + [pltpu.SMEM(fold_pair.shape, jnp.int32), pltpu.SemaphoreType.DMA((5,))],
        compiler_params=params(GRANT),
        name="prep",
    )(ocean_state, diffusivity, depth_levels, cotangent, fold_pair)

    rb = lax.ppermute(send, "lon", swap_pairs(lon_count, 1))
    ra = lax.ppermute(send, "lon", swap_pairs(lon_count, 0))

    entries = active_index.reshape(-1, COLS)
    first_taps = first_weight.transpose(0, 2, 1)

    pla, plb, plc, ce = pl.pallas_call(
        mid_kernel,
        out_shape=(block, block, block, shape((PACK, COLS), BF16)),
        in_specs=[smem()] + vmem(4),
        out_specs=tuple(vmem(4)),
        compiler_params=params(GRANT),
        name="mid",
    )(scal, send, bottom, ra, rb)

    near_a = [(i * lat_count + a, i * lat_count + b) for i in range(lon_count) for a, b in swap_pairs(lat_count, 0)]
    near_b = [
        (i * lat_count + a, i * lat_count + b) for i in range(lon_count) for a, b in swap_pairs(lat_count - 1, 1)
    ]
    turns = lon_count // 2

    def exchange(q, second):
        def run(pla, plb, plc):
            rlb = lax.ppermute(plb, BOTH, near_b + fold_pairs(lon_count, lat_count, q))
            if second:
                rlb = rlb + lax.ppermute(plc, BOTH, near_b + fold_pairs(lon_count, lat_count, (q + 1) % turns))
            return rlb, lax.ppermute(pla, BOTH, near_a)

        return run

    branches = [exchange(q, second) for q in range(turns) for second in (False, True)]
    rlb, rla = lax.switch(turn.reshape(()), branches, pla, plb, plc)

    new_state, closure, active = run_main(
        row_total, own, grad, ce, rla, rlb, first_taps, mix_weight, last_weight, entries
    )

    halves, cores, quads = 2, 2, 4
    inner = lon_count // halves
    everyone = lon_count * lat_count
    assert inner // cores == lat_count // quads * halves == cores * quads == SHARE

    def place_of(d):
        lon_at, lat_at = divmod(d, lat_count)
        z_hi, low = divmod(lon_at, inner)
        return z_hi, low // cores, low % cores, lat_at // quads, lat_at % quads

    def grouped(kept):
        return groups_of(everyone, lambda d: tuple(place_of(d)[i] for i in kept))

    total = reduce_over(active, grouped((0, 1, 3)))
    total = reduce_over(shared(total), grouped((0, 2, 3, 4)))
    total = reduce_over(shared(total), grouped((1, 2, 4)))
    return new_state, closure, total.reshape(-1)


def solution(mesh):
    in_specs = (
        P(None, None, "lat", "lon"),
        P(None, "lat", "lon"),
        P("lat", "lon"),
        P(),
        P(),
        P(),
        P(),
        P(None, "lat", "lon"),
        P(),
    )
    out_specs = (P(None, None, "lat", "lon"), P(None, "lat", "lon"), P())
    body = functools.partial(on_device, mesh.shape["lon"], mesh.shape["lat"])
    return jax.shard_map(body, mesh=mesh, in_specs=in_specs, out_specs=out_specs, check_vma=False)
```

```python
import collections
import functools
import math

import jax
import jax.numpy as jnp
from jax import lax
from jax.experimental import pallas as pl
from jax.experimental.pallas import tpu as pltpu
from jax.sharding import PartitionSpec as P

coriolis_peak = 0.25
pressure_scale = 0.05
advect_scale = 0.25

LEV = 8
ROWS = 16
COLS = 128
HALO = 4
EXT = ROWS + 2 * HALO
WIDE = 2 * COLS
CH = 64
INS = 3 * LEV
OUTS = 2 * LEV
PACK = 48
TAPK = 80
FIRST = 9 * CH * INS
MIX = CH * CH
GRANT = 60
SHARE = 8
BOTH = ("lon", "lat")
F32 = jnp.float32
BF16 = jnp.bfloat16


def params(mib=48):
    return pltpu.CompilerParams(vmem_limit_bytes=mib * 1024 * 1024)


def vmem(count):
    return [pl.BlockSpec(memory_space=pltpu.VMEM)] * count


def smem():
    return pl.BlockSpec(memory_space=pltpu.SMEM)


def iota(shape, axis):
    return lax.broadcasted_iota(jnp.int32, shape, axis)


def prep_kernel(
    grad_scale, col_total, lat_count, state_hbm, kappa_hbm, depth_hbm, cot_hbm, fold_hbm,
    own, grad, send, bottom, scal, turn, state, kappa, depth, cot, fold, sems,
):
    lat, lon = lax.axis_index("lat"), lax.axis_index("lon")
    pairs = ((state_hbm, state), (kappa_hbm, kappa), (depth_hbm, depth), (cot_hbm, cot), (fold_hbm, fold))
    copies = [pltpu.make_async_copy(a, b, sems.at[i]) for i, (a, b) in enumerate(pairs)]
    for copy in copies:
        copy.start()
    for copy in copies:
        copy.wait()
    folded = lax.rem(fold[0] + col_total - 3, col_total)
    rel = lax.rem(folded, WIDE) + 3
    scal[0] = lax.rem(lon, 2)
    scal[1] = rel
    scal[2] = (lax.rem(lat, 2) == 0).astype(jnp.int32)
    scal[3] = (lat == lat_count - 1).astype(jnp.int32)
    turn[0] = 2 * lax.div(folded, WIDE) + (rel + 4 >= WIDE).astype(jnp.int32)
    level = iota((LEV, COLS), 0)
    lane = iota((PACK, COLS), 1)
    fields = [jnp.swapaxes(state[f], 0, 1) for f in range(3)]
    kap = jnp.swapaxes(kappa[...], 0, 1)
    cots = jnp.swapaxes(cot[...].astype(F32), 0, 1)
    packed = jnp.zeros((PACK, COLS), F32)
    for r in range(ROWS):
        mask = (level < depth[r : r + 1, :]).astype(F32)
        row = jnp.concatenate([fields[f][r] * mask for f in range(3)] + [kap[r] * mask], axis=0)
        out_grad = grad_scale * jnp.concatenate([mask, mask], axis=0) * cots[r]
        own[r] = row
        grad[r] = out_grad.astype(BF16)
        both = jnp.concatenate([row, out_grad], axis=0)
        if r < HALO:
            bottom[r] = both.astype(BF16)
        if r >= ROWS - HALO:
            send[r - (ROWS - HALO)] = both.astype(BF16)
        moved = pltpu.roll(both, 8 * r, 1) if r else both
        here = ((lane - 8 * r + 4 + COLS) & (COLS - 1)) < 8
        packed = jnp.where(here, moved, packed)
    send[HALO] = packed.astype(BF16)


def mid_kernel(scal, own_top, own_bottom, ra, rb, pla, plb, plc, corner):
    core, rel, even, at_top = scal[0], scal[1], scal[2], scal[3] == 1
    lane = iota((PACK, COLS), 1)
    first_core = core == 0
    ea, eb = ra[HALO].astype(F32), rb[HALO].astype(F32)
    east_edge = jnp.where(first_core, ea, eb)
    west_edge = jnp.where(first_core, eb, ea)
    ce = jnp.where((lane & 7) < 4, east_edge, west_edge).astype(BF16)
    corner[...] = ce
    is_even = even == 1
    for k in range(HALO):
        up, down = own_top[k].astype(F32), own_bottom[k].astype(F32)
        pla[k] = jnp.where(is_even, up, down).astype(BF16)
        plb[k] = jnp.where(is_even, down, up).astype(BF16)
    pla[HALO] = ce
    plb[HALO] = ce

    @pl.when(jnp.logical_not(at_top))
    def _():
        plc[...] = jnp.zeros_like(plc)

    @pl.when(at_top)
    def _():
        fold_windows(first_core, rel, own_top, ra, rb, plb, plc)


def fold_windows(first_core, rel, own_top, ra, rb, f1, f2):
    lane = iota((PACK, COLS), 1)
    rows_a = ra[:HALO].astype(F32).reshape(HALO * PACK, COLS)
    rows_b = rb[:HALO].astype(F32).reshape(HALO * PACK, COLS)
    west = jnp.where(first_core, rows_b, rows_a).astype(BF16)
    east = jnp.where(first_core, rows_a, rows_b).astype(BF16)
    window = jnp.concatenate([west, own_top[:HALO].reshape(HALO * PACK, COLS), east], axis=1)
    src = iota((3 * COLS, WIDE), 0) - COLS
    t = iota((3 * COLS, WIDE), 1)
    q = t & 7
    target = jnp.where(t < COLS, t, jnp.where(q < 4, COLS + q, q - 8))
    chan = iota((PACK, COLS), 0)
    sign = jnp.where(chan < 2 * LEV, -1.0, jnp.where(chan < 4 * LEV, 1.0, 0.0)).astype(F32)
    slot = ((lane + 4) >> 3) & (ROWS - 1)
    for out, offset, least in ((f1, 0, -COLS), (f2, WIDE, 0)):
        pick = (src == rel - offset - target) & (src >= least)
        moved = jnp.dot(window, pick.astype(F32).astype(BF16), preferred_element_type=F32)
        ext = jnp.zeros((PACK, COLS), F32)
        for k in range(HALO):
            at = (HALO - 1 - k) * PACK
            out[k] = (moved[at : at + PACK, :COLS] * sign).astype(BF16)
            ext = jnp.where(slot == k, moved[at : at + PACK, COLS:], ext)
        out[HALO] = (ext * sign).astype(BF16)


def sigmoid(x):
    return 0.5 * jnp.tanh(0.5 * x) + 0.5


def placed_entries(active_index):
    def split(x, by):
        whole = lax.div(x, jnp.full_like(x, by))
        return whole, x - whole * by

    n = active_index
    k, rem = split(n, CH * INS)
    (dy, dx), (o, c) = split(k, 3), split(rem, INS)
    hi_a, lo_a = dy * TAPK + dx * INS + c, o
    o, c = split(n - FIRST, CH)
    hi_b, lo_b = 9 * OUTS + c, CH + o
    k, rem = split(n - FIRST - MIX, OUTS * CH)
    (dy, dx), (o, c) = split(k, 3), split(rem, CH)
    hi_c, lo_c = (2 - dy) * PACK + dx * OUTS + o, CH + c
    in_a, in_b = n < FIRST, n < FIRST + MIX
    hi = jnp.where(in_a, hi_a, jnp.where(in_b, hi_b, hi_c))
    lo = jnp.where(in_a, lo_a, jnp.where(in_b, lo_b, lo_c))
    return hi, lo


def main_kernel(
    row_total, own, grad, ce, rla, rlb, first_hbm, mix_hbm, last_hbm, entries_hbm,
    state_out, closure_out, active_out,
    z0, z1, kxe, kxn, pres, gx, x3, g3, ybuf, acc_first, acc_rest, picked,
    first_taps, mix, last, entries, w1, wmt, wl, wb, hi, lo, spin, sems,
):
    pairs = ((first_hbm, first_taps), (mix_hbm, mix), (last_hbm, last), (entries_hbm, entries))
    copies = [pltpu.make_async_copy(a, b, sems.at[i]) for i, (a, b) in enumerate(pairs)]
    for copy in copies:
        copy.start()
    lat = lax.axis_index("lat")
    even = lax.rem(lat, 2) == 0
    first_row = lat * ROWS - HALO
    at_row = first_row + iota((EXT, COLS), 0)
    mirrored = jnp.where(at_row >= row_total, 2 * row_total - 1 - at_row, at_row)
    spin[...] = coriolis_peak * jnp.sin(math.pi * (mirrored.astype(F32) + 0.5) / row_total - 0.5 * math.pi)

    def valid(y):
        return jnp.where((first_row + y >= 0) & (first_row + y < row_total), 1.0, 0.0)


    def place(y, left, corner_pack, slot):
        shift = (COLS - 8 * slot) % COLS
        right = pltpu.roll(corner_pack, shift, 1) if shift else corner_pack
        z0[y, :, :COLS] = left[: 4 * LEV]
        z0[y, :, COLS:] = right[: 4 * LEV]
        gx[y, :, :COLS] = left[4 * LEV :]
        gx[y, :, COLS:] = right[4 * LEV :]

    def south(k):
        return jnp.where(even, rlb[k].astype(F32), rla[k].astype(F32))

    def north(k):
        return jnp.where(even, rla[k].astype(F32), rlb[k].astype(F32))

    south_edge, north_edge, own_edge = south(HALO), north(HALO), ce[...].astype(F32)
    for k in range(HALO):
        place(k, south(k), south_edge, ROWS - HALO + k)
        place(HALO + ROWS + k, north(k), north_edge, k)
    for r in range(ROWS):
        full = jnp.concatenate([own[r], grad[r].astype(F32)], axis=0)
        place(HALO + r, full, own_edge, r)

    def east(x):
        return pltpu.roll(x, WIDE - 1, 1)

    def west(x):
        return pltpu.roll(x, 1, 1)

    level = iota((LEV, WIDE), 0)

    def depth_sum(x):
        for s in (1, 2, 4):
            x = x + jnp.where(level >= s, pltpu.roll(x, s, 0), 0.0)
        return x

    U, V, T, K = (slice(LEV * i, LEV * (i + 1)) for i in range(4))

    def coefficients(y, _):
        k = z0[y, K]
        kxe[y] = jnp.sqrt(k * east(k))
        kxn[y] = jnp.sqrt(k * z0[jnp.minimum(y + 1, EXT - 1), K])
        pres[y] = pressure_scale * depth_sum(z0[y, T])
        return 0

    lax.fori_loop(0, EXT, coefficients, 0, unroll=24)

    def step(src, dst, y):
        ke, kn, ks = kxe[y], kxn[y], kxn[y - 1]
        u, v, t = src[y, U], src[y, V], src[y, T]
        wet = (z0[y, K] > 0).astype(F32)
        row = spin[pl.ds(y, 1), :]
        f = jnp.concatenate([row, row], axis=1)

        def diffuse(z, zn, zs):
            flux = ke * (east(z) - z)
            return flux - west(flux) + kn * (zn - z) + ks * (zs - z)

        p = pres[y]
        un, us = src[y + 1, U], src[y - 1, U]
        vn, vs = src[y + 1, V], src[y - 1, V]
        tn, ts = src[y + 1, T], src[y - 1, T]
        du = f * v - 0.5 * (east(p) - west(p))
        dv = -f * u - 0.5 * (pres[y + 1] - pres[y - 1])
        dt = (-advect_scale * 0.5) * (u * (east(t) - west(t)) + v * (tn - ts))
        dst[y, U] = wet * (u + du + diffuse(u, un, us))
        dst[y, V] = wet * (v + dv + diffuse(v, vn, vs))
        dst[y, T] = wet * (t + dt + diffuse(t, tn, ts))

    def first_step(i, _):
        step(z0, z1, i)
        return 0

    lax.fori_loop(1, EXT - 1, first_step, 0, unroll=11)

    def second_pressure(y, _):
        pres[y] = pressure_scale * depth_sum(z1[y, T])
        return 0

    lax.fori_loop(1, EXT - 1, second_pressure, 0, unroll=22)

    zero_rows = jnp.zeros((TAPK - 3 * INS, COLS), F32)

    def second_step(y, _):
        step(z1, z0, y)
        x = z0[y, :INS] * valid(y)
        taps = jnp.concatenate([west(x)[:, :COLS], x[:, :COLS], east(x)[:, :COLS], zero_rows], axis=0)
        x3[pl.ds(pl.multiple_of(TAPK * y, 16), TAPK), :] = taps.astype(BF16)
        g = gx[y]
        tap_g = jnp.concatenate([east(g), g, west(g)], axis=0)[:, :COLS]
        g3[pl.ds(pl.multiple_of(PACK * y, 16), PACK), :] = tap_g.astype(BF16)
        return 0

    lax.fori_loop(2, EXT - 2, second_step, 0, unroll=5)
    new = z0[HALO : HALO + ROWS, :INS, :COLS]
    for f in range(3):
        state_out[f] = jnp.swapaxes(new[:, LEV * f : LEV * (f + 1), :], 0, 1)

    for copy in copies:
        copy.wait()
    pieces = []
    for k in range(9):
        pieces.append(first_taps[k].astype(F32))
        if k % 3 == 2:
            pieces.append(jnp.zeros((TAPK - 3 * INS, CH), F32))
    w1[...] = jnp.concatenate(pieces, axis=0).T.astype(BF16)
    wmt[...] = mix[...].astype(F32).T.astype(BF16)
    taps_of = [last[k].astype(F32) for k in range(9)]
    wl[...] = jnp.concatenate(taps_of, axis=0).astype(BF16)
    wb[...] = jnp.concatenate(taps_of[6:] + taps_of[3:6] + taps_of[:3], axis=0).T.astype(BF16)
    hi[...], lo[...] = placed_entries(entries[...])

    def hidden(taps):
        pre1 = jnp.dot(w1[...], taps, preferred_element_type=F32)
        s1 = sigmoid(pre1)
        h1 = (pre1 * s1).astype(BF16)
        pre2 = jnp.dot(mix[...], h1, preferred_element_type=F32)
        s2 = sigmoid(pre2)
        return pre1, s1, h1, pre2, s2, pre2 * s2

    def two_rows(ref, depth, y, z):
        return jnp.concatenate(
            [ref[pl.ds(pl.multiple_of(depth * (r - 1), 16), 3 * depth), :] for r in (y, z)], axis=1
        )

    def spread(h2):
        return jnp.dot(wl[...], h2.astype(BF16), preferred_element_type=F32)

    lane = iota((INS, COLS), 1)
    columns = [jnp.zeros((INS, COLS), F32)] * 3
    for y in range(2, EXT - 2):
        x = z0[y, :INS] * valid(y)
        inner, outer = x[:, :COLS], x[:, COLS:]
        sides = (jnp.where(lane == COLS - 1, inner, outer), outer, jnp.where(lane == 0, inner, outer))
        for d in range(3):
            moved = pltpu.roll(sides[d], 2 * y + 2 - d, 1)
            columns[d] = jnp.where((lane >> 1) == y, moved, columns[d])
    side_taps = []
    for shift in (2, 0, COLS - 2):
        side_taps += [pltpu.roll(c, shift, 1) if shift else c for c in columns] + [zero_rows]
    side_row = first_row + (iota((CH, COLS), 1) >> 1)
    side_valid = ((side_row >= 0) & (side_row < row_total)).astype(F32)
    side = spread(hidden(jnp.concatenate(side_taps, axis=0).astype(BF16))[5] * side_valid)
    side_sum = []
    for d in (0, 2):
        parts = [side[OUTS * (3 * k + d) : OUTS * (3 * k + d + 1)] for k in range(3)]
        side_sum.append(pltpu.roll(parts[0], 2, 1) + parts[1] + pltpu.roll(parts[2], COLS - 2, 1))

    low, high = HALO - 1, HALO + ROWS
    h2 = hidden(two_rows(x3, TAPK, low, high))[5]
    ends = spread(jnp.concatenate([h2[:, :COLS] * valid(low), h2[:, COLS:] * valid(high)], axis=1))
    ybuf[low] = ends[:, :COLS]
    ybuf[high] = ends[:, COLS:]
    acc_first[...] = jnp.zeros_like(acc_first)
    acc_rest[...] = jnp.zeros_like(acc_rest)
    nt = (((1,), (1,)), ((), ()))

    def both_ways(i, _):
        y = HALO + 2 * i
        taps = two_rows(x3, TAPK, y, y + 1)
        pre1, s1, h1, pre2, s2, act = hidden(taps)
        h2 = act.astype(BF16)
        out = spread(h2)
        ybuf[y] = out[:, :COLS]
        ybuf[y + 1] = out[:, COLS:]
        g9 = two_rows(g3, PACK, y, y + 1)
        back2 = jnp.dot(wb[...], g9, preferred_element_type=F32)
        d2 = (back2 * (s2 * (1.0 + pre2 * (1.0 - s2)))).astype(BF16)
        back1 = jnp.dot(wmt[...], d2, preferred_element_type=F32)
        d1 = (back1 * (s1 * (1.0 + pre1 * (1.0 - s1)))).astype(BF16)
        acc_first[:, : 3 * TAPK] += lax.dot_general(d1, taps, nt, preferred_element_type=F32)
        acc_rest[:, : 9 * OUTS + CH] += lax.dot_general(
            jnp.concatenate([h2, d2], axis=0), jnp.concatenate([g9, h1], axis=0), nt, preferred_element_type=F32
        )
        return 0

    lax.fori_loop(0, ROWS // 2, both_ways, 0, unroll=8)

    closed = []
    lane = iota((OUTS, COLS), 1)
    for r in range(ROWS):
        y = HALO + r
        part = [
            ybuf[y - 1, OUTS * d : OUTS * (d + 1)]
            + ybuf[y, OUTS * (3 + d) : OUTS * (4 + d)]
            + ybuf[y + 1, OUTS * (6 + d) : OUTS * (7 + d)]
            for d in range(3)
        ]
        from_west = jnp.where(lane == 0, pltpu.roll(side_sum[0], COLS - 2 * y, 1), pltpu.roll(part[0], 1, 1))
        from_east = jnp.where(
            lane == COLS - 1, pltpu.roll(side_sum[1], COLS - 2 - 2 * y, 1), pltpu.roll(part[2], COLS - 1, 1)
        )
        wet = (own[r, K] > 0).astype(F32)
        closed.append(jnp.concatenate([wet, wet], axis=0) * (from_west + part[1] + from_east))
    closure_out[...] = jnp.swapaxes(jnp.stack(closed), 0, 1).astype(BF16)

    is_last = iota((CH, WIDE), 1) < 9 * OUTS
    rest = jnp.where(is_last, acc_rest[:CH], acc_rest[CH:])
    table = jnp.concatenate([acc_first[...], rest], axis=0).astype(BF16)
    column = iota((WIDE, WIDE), 0)
    line = iota((2 * CH, WIDE), 0)

    def choose(c, _):
        at_hi = jnp.concatenate([hi[pl.ds(2 * c, 1), :], hi[pl.ds(2 * c + 1, 1), :]], axis=1)
        at_lo = jnp.concatenate([lo[pl.ds(2 * c, 1), :], lo[pl.ds(2 * c + 1, 1), :]], axis=1)
        hot = (column == at_hi).astype(F32).astype(BF16)
        found = jnp.dot(table, hot, preferred_element_type=F32)
        value = jnp.sum(jnp.where(line == at_lo, found, 0.0), axis=0, keepdims=True)
        picked[pl.ds(2 * c, 1), :] = value[:, :COLS]
        picked[pl.ds(2 * c + 1, 1), :] = value[:, COLS:]
        return 0

    lax.fori_loop(0, hi.shape[0] // 2, choose, 0, unroll=8)
    chosen = picked[...].astype(BF16)
    for k in range(SHARE):
        active_out[k] = chosen


def swap_pairs(count, start):
    out = []
    for i in range(start, count - 1 + start, 2):
        a, b = i % count, (i + 1) % count
        out += [(a, b), (b, a)]
    return out


def fold_pairs(lon_count, lat_count, q):
    row = lat_count - 1
    return [(i * lat_count + row, ((2 * q - i) % lon_count) * lat_count + row) for i in range(lon_count)]


def groups_of(count, key):
    out = collections.OrderedDict()
    for i in range(count):
        out.setdefault(key(i), []).append(i)
    return list(out.values())


def reduce_over(shares, groups):
    arrived = lax.all_to_all(shares, BOTH, 0, 0, axis_index_groups=groups)
    return jnp.sum(arrived.astype(F32), axis=0)


def shared(x):
    return jnp.broadcast_to(x.astype(BF16)[None], (SHARE,) + x.shape)


def run_main(row_total, *args):
    shape = jax.ShapeDtypeStruct
    lines = args[-1].shape[0]
    return pl.pallas_call(
        functools.partial(main_kernel, row_total),
        out_shape=(
            shape((3, LEV, ROWS, COLS), F32),
            shape((OUTS, ROWS, COLS), BF16),
            shape((SHARE, lines, COLS), BF16),
        ),
        in_specs=vmem(5) + [pl.BlockSpec(memory_space=pltpu.HBM)] * 4,
        out_specs=tuple(vmem(3)),
        scratch_shapes=[
            pltpu.VMEM((EXT, 4 * LEV, WIDE), F32),
            pltpu.VMEM((EXT, 4 * LEV, WIDE), F32),
            pltpu.VMEM((EXT, LEV, WIDE), F32),
            pltpu.VMEM((EXT, LEV, WIDE), F32),
            pltpu.VMEM((EXT, LEV, WIDE), F32),
            pltpu.VMEM((EXT, OUTS, WIDE), F32),
            pltpu.VMEM((EXT * TAPK, COLS), BF16),
            pltpu.VMEM((EXT * PACK, COLS), BF16),
            pltpu.VMEM((EXT, 9 * OUTS, COLS), F32),
            pltpu.VMEM((CH, WIDE), F32),
            pltpu.VMEM((2 * CH, WIDE), F32),
            pltpu.VMEM((lines, COLS), F32),
        ]
        + [pltpu.VMEM(x.shape, x.dtype) for x in args[-4:]]
        + [
            pltpu.VMEM((CH, 3 * TAPK), BF16),
            pltpu.VMEM((CH, CH), BF16),
            pltpu.VMEM((9 * OUTS, CH), BF16),
            pltpu.VMEM((CH, 9 * OUTS), BF16),
            pltpu.VMEM((lines, COLS), jnp.int32),
            pltpu.VMEM((lines, COLS), jnp.int32),
            pltpu.VMEM((EXT, COLS), F32),
            pltpu.SemaphoreType.DMA((4,)),
        ],
        compiler_params=params(GRANT),
        name="main",
    )(*args)


def on_device(
    lon_count, lat_count,
    ocean_state, diffusivity, depth_levels, fold_pair, first_weight, mix_weight, last_weight, cotangent, active_index,
):
    lat, lon = lax.axis_index("lat"), lax.axis_index("lon")
    row_total, col_total = ROWS * lat_count, COLS * lon_count
    shape = jax.ShapeDtypeStruct
    block = shape((HALO + 1, PACK, COLS), BF16)
    own, grad, send, bottom, scal, turn = pl.pallas_call(
        functools.partial(prep_kernel, 1.0 / math.sqrt(row_total * col_total), col_total, lat_count),
        out_shape=(
            shape((ROWS, 4 * LEV, COLS), F32),
            shape((ROWS, OUTS, COLS), BF16),
            block,
            shape((HALO, PACK, COLS), BF16),
            shape((4,), jnp.int32),
            shape((1,), jnp.int32),
        ),
        in_specs=[pl.BlockSpec(memory_space=pltpu.HBM)] * 5,
        out_specs=tuple(vmem(4) + [smem()] * 2),
        scratch_shapes=[
            pltpu.VMEM(x.shape, x.dtype) for x in (ocean_state, diffusivity, depth_levels, cotangent)
        ]
        + [pltpu.SMEM(fold_pair.shape, jnp.int32), pltpu.SemaphoreType.DMA((5,))],
        compiler_params=params(GRANT),
        name="prep",
    )(ocean_state, diffusivity, depth_levels, cotangent, fold_pair)

    rb = lax.ppermute(send, "lon", swap_pairs(lon_count, 1))
    ra = lax.ppermute(send, "lon", swap_pairs(lon_count, 0))

    entries = active_index.reshape(-1, COLS)
    first_taps = first_weight.transpose(0, 2, 1)

    pla, plb, plc, ce = pl.pallas_call(
        mid_kernel,
        out_shape=(block, block, block, shape((PACK, COLS), BF16)),
        in_specs=[smem()] + vmem(4),
        out_specs=tuple(vmem(4)),
        compiler_params=params(GRANT),
        name="mid",
    )(scal, send, bottom, ra, rb)

    near_a = [(i * lat_count + a, i * lat_count + b) for i in range(lon_count) for a, b in swap_pairs(lat_count, 0)]
    near_b = [
        (i * lat_count + a, i * lat_count + b) for i in range(lon_count) for a, b in swap_pairs(lat_count - 1, 1)
    ]
    turns = lon_count // 2

    def exchange(q, second):
        def run(pla, plb, plc):
            rlb = lax.ppermute(plb, BOTH, near_b + fold_pairs(lon_count, lat_count, q))
            if second:
                rlb = rlb + lax.ppermute(plc, BOTH, near_b + fold_pairs(lon_count, lat_count, (q + 1) % turns))
            return rlb, lax.ppermute(pla, BOTH, near_a)

        return run

    branches = [exchange(q, second) for q in range(turns) for second in (False, True)]
    rlb, rla = lax.switch(turn.reshape(()), branches, pla, plb, plc)

    new_state, closure, active = run_main(
        row_total, own, grad, ce, rla, rlb, first_taps, mix_weight, last_weight, entries
    )

    halves, cores, quads = 2, 2, 4
    inner = lon_count // halves
    everyone = lon_count * lat_count
    assert inner // cores == lat_count // quads * halves == cores * quads == SHARE

    def place_of(d):
        lon_at, lat_at = divmod(d, lat_count)
        z_hi, low = divmod(lon_at, inner)
        return z_hi, low // cores, low % cores, lat_at // quads, lat_at % quads

    def grouped(kept):
        return groups_of(everyone, lambda d: tuple(place_of(d)[i] for i in kept))

    total = reduce_over(active, grouped((0, 1, 3)))
    total = reduce_over(shared(total), grouped((0, 2, 3, 4)))
    total = reduce_over(shared(total), grouped((1, 2, 4)))
    return new_state, closure, total.reshape(-1)


def solution(mesh):
    in_specs = (
        P(None, None, "lat", "lon"),
        P(None, "lat", "lon"),
        P("lat", "lon"),
        P(),
        P(),
        P(),
        P(),
        P(None, "lat", "lon"),
        P(),
    )
    out_specs = (P(None, None, "lat", "lon"), P(None, "lat", "lon"), P())
    body = functools.partial(on_device, mesh.shape["lon"], mesh.shape["lat"])
    return jax.shard_map(body, mesh=mesh, in_specs=in_specs, out_specs=out_specs, check_vma=False)
```

```python
import collections
import functools
import math

import jax
import jax.numpy as jnp
from jax import lax
from jax.experimental import pallas as pl
from jax.experimental.pallas import tpu as pltpu
from jax.sharding import PartitionSpec as P

coriolis_peak = 0.25
pressure_scale = 0.05
advect_scale = 0.25

LEV = 8
ROWS = 16
COLS = 128
HALO = 4
EXT = ROWS + 2 * HALO
WIDE = 2 * COLS
CH = 64
INS = 3 * LEV
OUTS = 2 * LEV
PACK = 48
STATE = 4 * LEV
TAPK = 80
FIRST = 9 * CH * INS
MIX = CH * CH
GRANT = 60
SHARE = 8
BOTH = ("lon", "lat")
F32 = jnp.float32
BF16 = jnp.bfloat16


def params(mib=48):
    return pltpu.CompilerParams(vmem_limit_bytes=mib * 1024 * 1024)


def vmem(count):
    return [pl.BlockSpec(memory_space=pltpu.VMEM)] * count


def smem():
    return pl.BlockSpec(memory_space=pltpu.SMEM)


def iota(shape, axis):
    return lax.broadcasted_iota(jnp.int32, shape, axis)


def prep_kernel(
    grad_scale, col_total, lat_count, state_hbm, kappa_hbm, depth_hbm, cot_hbm, fold_hbm,
    own, grad, send, top, bottom, scal, turn, state, kappa, depth, cot, fold, sems,
):
    lat, lon = lax.axis_index("lat"), lax.axis_index("lon")
    pairs = ((state_hbm, state), (kappa_hbm, kappa), (depth_hbm, depth), (cot_hbm, cot), (fold_hbm, fold))
    copies = [pltpu.make_async_copy(a, b, sems.at[i]) for i, (a, b) in enumerate(pairs)]
    for copy in copies:
        copy.start()
    for copy in copies:
        copy.wait()
    folded = lax.rem(fold[0] + col_total - 3, col_total)
    rel = lax.rem(folded, WIDE) + 3
    scal[0] = lax.rem(lon, 2)
    scal[1] = rel
    scal[2] = (lax.rem(lat, 2) == 0).astype(jnp.int32)
    scal[3] = (lat == lat_count - 1).astype(jnp.int32)
    turn[0] = 2 * lax.div(folded, WIDE) + (rel + 4 >= WIDE).astype(jnp.int32)
    level = iota((LEV, COLS), 0)
    lane = iota((PACK, COLS), 1)
    fields = [jnp.swapaxes(state[f], 0, 1) for f in range(3)]
    kap = jnp.swapaxes(kappa[...], 0, 1)
    cots = jnp.swapaxes(cot[...].astype(F32), 0, 1)
    packed = jnp.zeros((PACK, COLS), F32)
    for r in range(ROWS):
        mask = (level < depth[r : r + 1, :]).astype(F32)
        row = jnp.concatenate([fields[f][r] * mask for f in range(3)] + [kap[r] * mask], axis=0)
        out_grad = grad_scale * jnp.concatenate([mask, mask], axis=0) * cots[r]
        own[r] = row
        grad[r] = out_grad.astype(BF16)
        both = jnp.concatenate([row, out_grad], axis=0)
        if r < HALO:
            bottom[r] = both.astype(BF16)
        if r >= ROWS - HALO:
            k = r - (ROWS - HALO)
            top[k] = both.astype(BF16)
            send[STATE * k : STATE * (k + 1)] = row.astype(BF16)
        moved = pltpu.roll(both, 8 * r, 1) if r else both
        here = ((lane - 8 * r + 4 + COLS) & (COLS - 1)) < 8
        packed = jnp.where(here, moved, packed)
    send[STATE * HALO :] = packed.astype(BF16)


def mid_kernel(scal, own_top, own_bottom, ra, rb, pla, plb, plc, corner):
    core, rel, even, at_top = scal[0], scal[1], scal[2], scal[3] == 1
    lane = iota((PACK, COLS), 1)
    first_core = core == 0
    ea, eb = ra[STATE * HALO :].astype(F32), rb[STATE * HALO :].astype(F32)
    east_edge = jnp.where(first_core, ea, eb)
    west_edge = jnp.where(first_core, eb, ea)
    ce = jnp.where((lane & 7) < 4, east_edge, west_edge).astype(BF16)
    corner[...] = ce
    is_even = even == 1
    for k in range(HALO):
        up, down = own_top[k].astype(F32), own_bottom[k].astype(F32)
        pla[k] = jnp.where(is_even, up, down).astype(BF16)
        plb[k] = jnp.where(is_even, down, up).astype(BF16)
    pla[HALO] = ce
    plb[HALO] = ce

    @pl.when(jnp.logical_not(at_top))
    def _():
        plc[...] = jnp.zeros_like(plc)

    @pl.when(at_top)
    def _():
        fold_windows(first_core, rel, own_top, ra, rb, plb, plc)


def fold_windows(first_core, rel, own_top, ra, rb, f1, f2):
    lane = iota((PACK, COLS), 1)
    rows_a = ra[: STATE * HALO].astype(F32)
    rows_b = rb[: STATE * HALO].astype(F32)
    west = jnp.where(first_core, rows_b, rows_a).astype(BF16)
    east = jnp.where(first_core, rows_a, rows_b).astype(BF16)
    window = jnp.concatenate([west, own_top[:, :STATE].reshape(HALO * STATE, COLS), east], axis=1)
    src = iota((3 * COLS, WIDE), 0) - COLS
    t = iota((3 * COLS, WIDE), 1)
    q = t & 7
    target = jnp.where(t < COLS, t, jnp.where(q < 4, COLS + q, q - 8))
    chan = iota((PACK, COLS), 0)
    sign = jnp.where(chan < 2 * LEV, -1.0, jnp.where(chan < 4 * LEV, 1.0, 0.0)).astype(F32)
    slot = ((lane + 4) >> 3) & (ROWS - 1)
    rest = jnp.zeros((PACK - STATE, WIDE), F32)
    for out, offset, least in ((f1, 0, -COLS), (f2, WIDE, 0)):
        pick = (src == rel - offset - target) & (src >= least)
        moved = jnp.dot(window, pick.astype(F32).astype(BF16), preferred_element_type=F32)
        ext = jnp.zeros((PACK, COLS), F32)
        for k in range(HALO):
            at = (HALO - 1 - k) * STATE
            line = jnp.concatenate([moved[at : at + STATE], rest], axis=0)
            out[k] = (line[:, :COLS] * sign).astype(BF16)
            ext = jnp.where(slot == k, line[:, COLS:], ext)
        out[HALO] = (ext * sign).astype(BF16)


def sigmoid(x):
    return 0.5 * jnp.tanh(0.5 * x) + 0.5


def placed_entries(active_index):
    def split(x, by):
        whole = lax.div(x, jnp.full_like(x, by))
        return whole, x - whole * by

    n = active_index
    k, rem = split(n, CH * INS)
    (dy, dx), (o, c) = split(k, 3), split(rem, INS)
    hi_a, lo_a = dy * TAPK + dx * INS + c, o
    o, c = split(n - FIRST, CH)
    hi_b, lo_b = 9 * OUTS + c, CH + o
    k, rem = split(n - FIRST - MIX, OUTS * CH)
    (dy, dx), (o, c) = split(k, 3), split(rem, CH)
    hi_c, lo_c = (2 - dy) * PACK + dx * OUTS + o, CH + c
    in_a, in_b = n < FIRST, n < FIRST + MIX
    hi = jnp.where(in_a, hi_a, jnp.where(in_b, hi_b, hi_c))
    lo = jnp.where(in_a, lo_a, jnp.where(in_b, lo_b, lo_c))
    return hi, lo


def main_kernel(
    row_total, own, grad, ce, rla, rlb, first_hbm, mix_hbm, last_hbm, entries_hbm,
    state_out, closure_out, active_out,
    z0, z1, kxe, kxn, pres, gx, x3, g3, ybuf, acc_first, acc_rest, picked,
    first_taps, mix, last, entries, w1, wmt, wl, wb, hi, lo, spin, sems,
):
    pairs = ((first_hbm, first_taps), (mix_hbm, mix), (last_hbm, last), (entries_hbm, entries))
    copies = [pltpu.make_async_copy(a, b, sems.at[i]) for i, (a, b) in enumerate(pairs)]
    for copy in copies:
        copy.start()
    lat = lax.axis_index("lat")
    even = lax.rem(lat, 2) == 0
    first_row = lat * ROWS - HALO
    at_row = first_row + iota((EXT, COLS), 0)
    mirrored = jnp.where(at_row >= row_total, 2 * row_total - 1 - at_row, at_row)
    spin[...] = coriolis_peak * jnp.sin(math.pi * (mirrored.astype(F32) + 0.5) / row_total - 0.5 * math.pi)

    def valid(y):
        return jnp.where((first_row + y >= 0) & (first_row + y < row_total), 1.0, 0.0)


    def place(y, left, corner_pack, slot):
        shift = (COLS - 8 * slot) % COLS
        right = pltpu.roll(corner_pack, shift, 1) if shift else corner_pack
        z0[y, :, :COLS] = left[: 4 * LEV]
        z0[y, :, COLS:] = right[: 4 * LEV]
        gx[y, :, :COLS] = left[4 * LEV :]
        gx[y, :, COLS:] = right[4 * LEV :]

    def south(k):
        return jnp.where(even, rlb[k].astype(F32), rla[k].astype(F32))

    def north(k):
        return jnp.where(even, rla[k].astype(F32), rlb[k].astype(F32))

    south_edge, north_edge, own_edge = south(HALO), north(HALO), ce[...].astype(F32)
    for k in range(HALO):
        place(k, south(k), south_edge, ROWS - HALO + k)
        place(HALO + ROWS + k, north(k), north_edge, k)
    for r in range(ROWS):
        full = jnp.concatenate([own[r], grad[r].astype(F32)], axis=0)
        place(HALO + r, full, own_edge, r)

    def east(x):
        return pltpu.roll(x, WIDE - 1, 1)

    def west(x):
        return pltpu.roll(x, 1, 1)

    level = iota((LEV, WIDE), 0)

    def depth_sum(x):
        for s in (1, 2, 4):
            x = x + jnp.where(level >= s, pltpu.roll(x, s, 0), 0.0)
        return x

    U, V, T, K = (slice(LEV * i, LEV * (i + 1)) for i in range(4))

    def coefficients(y, _):
        k = z0[y, K]
        kxe[y] = jnp.sqrt(k * east(k))
        kxn[y] = jnp.sqrt(k * z0[jnp.minimum(y + 1, EXT - 1), K])
        pres[y] = pressure_scale * depth_sum(z0[y, T])
        return 0

    lax.fori_loop(0, EXT, coefficients, 0, unroll=24)

    def step(src, dst, y):
        ke, kn, ks = kxe[y], kxn[y], kxn[y - 1]
        u, v, t = src[y, U], src[y, V], src[y, T]
        wet = (z0[y, K] > 0).astype(F32)
        row = spin[pl.ds(y, 1), :]
        f = jnp.concatenate([row, row], axis=1)

        def diffuse(z, zn, zs):
            flux = ke * (east(z) - z)
            return flux - west(flux) + kn * (zn - z) + ks * (zs - z)

        p = pres[y]
        un, us = src[y + 1, U], src[y - 1, U]
        vn, vs = src[y + 1, V], src[y - 1, V]
        tn, ts = src[y + 1, T], src[y - 1, T]
        du = f * v - 0.5 * (east(p) - west(p))
        dv = -f * u - 0.5 * (pres[y + 1] - pres[y - 1])
        dt = (-advect_scale * 0.5) * (u * (east(t) - west(t)) + v * (tn - ts))
        dst[y, U] = wet * (u + du + diffuse(u, un, us))
        dst[y, V] = wet * (v + dv + diffuse(v, vn, vs))
        dst[y, T] = wet * (t + dt + diffuse(t, tn, ts))

    def first_step(i, _):
        step(z0, z1, i)
        return 0

    lax.fori_loop(1, EXT - 1, first_step, 0, unroll=11)

    def second_pressure(y, _):
        pres[y] = pressure_scale * depth_sum(z1[y, T])
        return 0

    lax.fori_loop(1, EXT - 1, second_pressure, 0, unroll=22)

    zero_rows = jnp.zeros((TAPK - 3 * INS, COLS), F32)

    def second_step(y, _):
        step(z1, z0, y)
        x = z0[y, :INS] * valid(y)
        taps = jnp.concatenate([west(x)[:, :COLS], x[:, :COLS], east(x)[:, :COLS], zero_rows], axis=0)
        x3[pl.ds(pl.multiple_of(TAPK * y, 16), TAPK), :] = taps.astype(BF16)
        g = gx[y]
        tap_g = jnp.concatenate([east(g), g, west(g)], axis=0)[:, :COLS]
        g3[pl.ds(pl.multiple_of(PACK * y, 16), PACK), :] = tap_g.astype(BF16)
        return 0

    lax.fori_loop(2, EXT - 2, second_step, 0, unroll=5)
    new = z0[HALO : HALO + ROWS, :INS, :COLS]
    for f in range(3):
        state_out[f] = jnp.swapaxes(new[:, LEV * f : LEV * (f + 1), :], 0, 1)

    for copy in copies:
        copy.wait()
    pieces = []
    for k in range(9):
        pieces.append(first_taps[k].astype(F32))
        if k % 3 == 2:
            pieces.append(jnp.zeros((TAPK - 3 * INS, CH), F32))
    w1[...] = jnp.concatenate(pieces, axis=0).T.astype(BF16)
    wmt[...] = mix[...].astype(F32).T.astype(BF16)
    taps_of = [last[k].astype(F32) for k in range(9)]
    wl[...] = jnp.concatenate(taps_of, axis=0).astype(BF16)
    wb[...] = jnp.concatenate(taps_of[6:] + taps_of[3:6] + taps_of[:3], axis=0).T.astype(BF16)
    hi[...], lo[...] = placed_entries(entries[...])

    def hidden(taps):
        pre1 = jnp.dot(w1[...], taps, preferred_element_type=F32)
        s1 = sigmoid(pre1)
        h1 = (pre1 * s1).astype(BF16)
        pre2 = jnp.dot(mix[...], h1, preferred_element_type=F32)
        s2 = sigmoid(pre2)
        return pre1, s1, h1, pre2, s2, pre2 * s2

    def two_rows(ref, depth, y, z):
        return jnp.concatenate(
            [ref[pl.ds(pl.multiple_of(depth * (r - 1), 16), 3 * depth), :] for r in (y, z)], axis=1
        )

    def spread(h2):
        return jnp.dot(wl[...], h2.astype(BF16), preferred_element_type=F32)

    lane = iota((INS, COLS), 1)
    columns = [jnp.zeros((INS, COLS), F32)] * 3
    for y in range(2, EXT - 2):
        x = z0[y, :INS] * valid(y)
        inner, outer = x[:, :COLS], x[:, COLS:]
        sides = (jnp.where(lane == COLS - 1, inner, outer), outer, jnp.where(lane == 0, inner, outer))
        for d in range(3):
            moved = pltpu.roll(sides[d], 2 * y + 2 - d, 1)
            columns[d] = jnp.where((lane >> 1) == y, moved, columns[d])
    side_taps = []
    for shift in (2, 0, COLS - 2):
        side_taps += [pltpu.roll(c, shift, 1) if shift else c for c in columns] + [zero_rows]
    side_row = first_row + (iota((CH, COLS), 1) >> 1)
    side_valid = ((side_row >= 0) & (side_row < row_total)).astype(F32)
    side = spread(hidden(jnp.concatenate(side_taps, axis=0).astype(BF16))[5] * side_valid)
    side_sum = []
    for d in (0, 2):
        parts = [side[OUTS * (3 * k + d) : OUTS * (3 * k + d + 1)] for k in range(3)]
        side_sum.append(pltpu.roll(parts[0], 2, 1) + parts[1] + pltpu.roll(parts[2], COLS - 2, 1))

    low, high = HALO - 1, HALO + ROWS
    h2 = hidden(two_rows(x3, TAPK, low, high))[5]
    ends = spread(jnp.concatenate([h2[:, :COLS] * valid(low), h2[:, COLS:] * valid(high)], axis=1))
    ybuf[low] = ends[:, :COLS]
    ybuf[high] = ends[:, COLS:]
    acc_first[...] = jnp.zeros_like(acc_first)
    acc_rest[...] = jnp.zeros_like(acc_rest)
    nt = (((1,), (1,)), ((), ()))

    def both_ways(i, _):
        y = HALO + 2 * i
        taps = two_rows(x3, TAPK, y, y + 1)
        pre1, s1, h1, pre2, s2, act = hidden(taps)
        h2 = act.astype(BF16)
        out = spread(h2)
        ybuf[y] = out[:, :COLS]
        ybuf[y + 1] = out[:, COLS:]
        g9 = two_rows(g3, PACK, y, y + 1)
        back2 = jnp.dot(wb[...], g9, preferred_element_type=F32)
        d2 = (back2 * (s2 * (1.0 + pre2 * (1.0 - s2)))).astype(BF16)
        back1 = jnp.dot(wmt[...], d2, preferred_element_type=F32)
        d1 = (back1 * (s1 * (1.0 + pre1 * (1.0 - s1)))).astype(BF16)
        acc_first[:, : 3 * TAPK] += lax.dot_general(d1, taps, nt, preferred_element_type=F32)
        acc_rest[:, : 9 * OUTS + CH] += lax.dot_general(
            jnp.concatenate([h2, d2], axis=0), jnp.concatenate([g9, h1], axis=0), nt, preferred_element_type=F32
        )
        return 0

    lax.fori_loop(0, ROWS // 2, both_ways, 0, unroll=8)

    closed = []
    lane = iota((OUTS, COLS), 1)
    for r in range(ROWS):
        y = HALO + r
        part = [
            ybuf[y - 1, OUTS * d : OUTS * (d + 1)]
            + ybuf[y, OUTS * (3 + d) : OUTS * (4 + d)]
            + ybuf[y + 1, OUTS * (6 + d) : OUTS * (7 + d)]
            for d in range(3)
        ]
        from_west = jnp.where(lane == 0, pltpu.roll(side_sum[0], COLS - 2 * y, 1), pltpu.roll(part[0], 1, 1))
        from_east = jnp.where(
            lane == COLS - 1, pltpu.roll(side_sum[1], COLS - 2 - 2 * y, 1), pltpu.roll(part[2], COLS - 1, 1)
        )
        wet = (own[r, K] > 0).astype(F32)
        closed.append(jnp.concatenate([wet, wet], axis=0) * (from_west + part[1] + from_east))
    closure_out[...] = jnp.swapaxes(jnp.stack(closed), 0, 1).astype(BF16)

    is_last = iota((CH, WIDE), 1) < 9 * OUTS
    rest = jnp.where(is_last, acc_rest[:CH], acc_rest[CH:])
    table = jnp.concatenate([acc_first[...], rest], axis=0).astype(BF16)
    column = iota((WIDE, WIDE), 0)
    line = iota((2 * CH, WIDE), 0)

    def choose(c, _):
        at_hi = jnp.concatenate([hi[pl.ds(2 * c, 1), :], hi[pl.ds(2 * c + 1, 1), :]], axis=1)
        at_lo = jnp.concatenate([lo[pl.ds(2 * c, 1), :], lo[pl.ds(2 * c + 1, 1), :]], axis=1)
        hot = (column == at_hi).astype(F32).astype(BF16)
        found = jnp.dot(table, hot, preferred_element_type=F32)
        value = jnp.sum(jnp.where(line == at_lo, found, 0.0), axis=0, keepdims=True)
        picked[pl.ds(2 * c, 1), :] = value[:, :COLS]
        picked[pl.ds(2 * c + 1, 1), :] = value[:, COLS:]
        return 0

    lax.fori_loop(0, hi.shape[0] // 2, choose, 0, unroll=8)
    chosen = picked[...].astype(BF16)
    for k in range(SHARE):
        active_out[k] = chosen


def swap_pairs(count, start):
    out = []
    for i in range(start, count - 1 + start, 2):
        a, b = i % count, (i + 1) % count
        out += [(a, b), (b, a)]
    return out


def fold_pairs(lon_count, lat_count, q):
    row = lat_count - 1
    return [(i * lat_count + row, ((2 * q - i) % lon_count) * lat_count + row) for i in range(lon_count)]


def groups_of(count, key):
    out = collections.OrderedDict()
    for i in range(count):
        out.setdefault(key(i), []).append(i)
    return list(out.values())


def reduce_over(shares, groups):
    arrived = lax.all_to_all(shares, BOTH, 0, 0, axis_index_groups=groups)
    return jnp.sum(arrived.astype(F32), axis=0)


def shared(x):
    return jnp.broadcast_to(x.astype(BF16)[None], (SHARE,) + x.shape)


def run_main(row_total, *args):
    shape = jax.ShapeDtypeStruct
    lines = args[-1].shape[0]
    return pl.pallas_call(
        functools.partial(main_kernel, row_total),
        out_shape=(
            shape((3, LEV, ROWS, COLS), F32),
            shape((OUTS, ROWS, COLS), BF16),
            shape((SHARE, lines, COLS), BF16),
        ),
        in_specs=vmem(5) + [pl.BlockSpec(memory_space=pltpu.HBM)] * 4,
        out_specs=tuple(vmem(3)),
        scratch_shapes=[
            pltpu.VMEM((EXT, 4 * LEV, WIDE), F32),
            pltpu.VMEM((EXT, 4 * LEV, WIDE), F32),
            pltpu.VMEM((EXT, LEV, WIDE), F32),
            pltpu.VMEM((EXT, LEV, WIDE), F32),
            pltpu.VMEM((EXT, LEV, WIDE), F32),
            pltpu.VMEM((EXT, OUTS, WIDE), F32),
            pltpu.VMEM((EXT * TAPK, COLS), BF16),
            pltpu.VMEM((EXT * PACK, COLS), BF16),
            pltpu.VMEM((EXT, 9 * OUTS, COLS), F32),
            pltpu.VMEM((CH, WIDE), F32),
            pltpu.VMEM((2 * CH, WIDE), F32),
            pltpu.VMEM((lines, COLS), F32),
        ]
        + [pltpu.VMEM(x.shape, x.dtype) for x in args[-4:]]
        + [
            pltpu.VMEM((CH, 3 * TAPK), BF16),
            pltpu.VMEM((CH, CH), BF16),
            pltpu.VMEM((9 * OUTS, CH), BF16),
            pltpu.VMEM((CH, 9 * OUTS), BF16),
            pltpu.VMEM((lines, COLS), jnp.int32),
            pltpu.VMEM((lines, COLS), jnp.int32),
            pltpu.VMEM((EXT, COLS), F32),
            pltpu.SemaphoreType.DMA((4,)),
        ],
        compiler_params=params(GRANT),
        name="main",
    )(*args)


def on_device(
    lon_count, lat_count,
    ocean_state, diffusivity, depth_levels, fold_pair, first_weight, mix_weight, last_weight, cotangent, active_index,
):
    lat, lon = lax.axis_index("lat"), lax.axis_index("lon")
    row_total, col_total = ROWS * lat_count, COLS * lon_count
    shape = jax.ShapeDtypeStruct
    block = shape((HALO + 1, PACK, COLS), BF16)
    own, grad, send, top, bottom, scal, turn = pl.pallas_call(
        functools.partial(prep_kernel, 1.0 / math.sqrt(row_total * col_total), col_total, lat_count),
        out_shape=(
            shape((ROWS, 4 * LEV, COLS), F32),
            shape((ROWS, OUTS, COLS), BF16),
            shape((HALO * STATE + PACK, COLS), BF16),
            shape((HALO, PACK, COLS), BF16),
            shape((HALO, PACK, COLS), BF16),
            shape((4,), jnp.int32),
            shape((1,), jnp.int32),
        ),
        in_specs=[pl.BlockSpec(memory_space=pltpu.HBM)] * 5,
        out_specs=tuple(vmem(5) + [smem()] * 2),
        scratch_shapes=[
            pltpu.VMEM(x.shape, x.dtype) for x in (ocean_state, diffusivity, depth_levels, cotangent)
        ]
        + [pltpu.SMEM(fold_pair.shape, jnp.int32), pltpu.SemaphoreType.DMA((5,))],
        compiler_params=params(GRANT),
        name="prep",
    )(ocean_state, diffusivity, depth_levels, cotangent, fold_pair)

    rb = lax.ppermute(send, "lon", swap_pairs(lon_count, 1))
    ra = lax.ppermute(send, "lon", swap_pairs(lon_count, 0))

    entries = active_index.reshape(-1, COLS)
    first_taps = first_weight.transpose(0, 2, 1)

    pla, plb, plc, ce = pl.pallas_call(
        mid_kernel,
        out_shape=(block, block, block, shape((PACK, COLS), BF16)),
        in_specs=[smem()] + vmem(4),
        out_specs=tuple(vmem(4)),
        compiler_params=params(GRANT),
        name="mid",
    )(scal, top, bottom, ra, rb)

    near_a = [(i * lat_count + a, i * lat_count + b) for i in range(lon_count) for a, b in swap_pairs(lat_count, 0)]
    near_b = [
        (i * lat_count + a, i * lat_count + b) for i in range(lon_count) for a, b in swap_pairs(lat_count - 1, 1)
    ]
    turns = lon_count // 2

    def exchange(q, second):
        def run(pla, plb, plc):
            rlb = lax.ppermute(plb, BOTH, near_b + fold_pairs(lon_count, lat_count, q))
            if second:
                rlb = rlb + lax.ppermute(plc, BOTH, near_b + fold_pairs(lon_count, lat_count, (q + 1) % turns))
            return rlb, lax.ppermute(pla, BOTH, near_a)

        return run

    branches = [exchange(q, second) for q in range(turns) for second in (False, True)]
    rlb, rla = lax.switch(turn.reshape(()), branches, pla, plb, plc)

    new_state, closure, active = run_main(
        row_total, own, grad, ce, rla, rlb, first_taps, mix_weight, last_weight, entries
    )

    halves, cores, quads = 2, 2, 4
    inner = lon_count // halves
    everyone = lon_count * lat_count
    assert inner // cores == lat_count // quads * halves == cores * quads == SHARE

    def place_of(d):
        lon_at, lat_at = divmod(d, lat_count)
        z_hi, low = divmod(lon_at, inner)
        return z_hi, low // cores, low % cores, lat_at // quads, lat_at % quads

    def grouped(kept):
        return groups_of(everyone, lambda d: tuple(place_of(d)[i] for i in kept))

    total = reduce_over(active, grouped((0, 1, 3)))
    total = reduce_over(shared(total), grouped((0, 2, 3, 4)))
    total = reduce_over(shared(total), grouped((1, 2, 4)))
    return new_state, closure, total.reshape(-1)


def solution(mesh):
    in_specs = (
        P(None, None, "lat", "lon"),
        P(None, "lat", "lon"),
        P("lat", "lon"),
        P(),
        P(),
        P(),
        P(),
        P(None, "lat", "lon"),
        P(),
    )
    out_specs = (P(None, None, "lat", "lon"), P(None, "lat", "lon"), P())
    body = functools.partial(on_device, mesh.shape["lon"], mesh.shape["lat"])
    return jax.shard_map(body, mesh=mesh, in_specs=in_specs, out_specs=out_specs, check_vma=False)
```
